32 devices in a mesh: dp: 4 (over y, x), row: 2 (over core), col: 4 (over z).
Axes of the slice: x: 2, y: 2, z: 4, core: 2. Of those that a mesh axis runs over, the one named last changes fastest.
Arguments:
- partials: bfloat16 [4, 2, 4, 2, 1024, 8192], P('dp', None, None, 'row', None, 'col'), may hold values from -40 to 40
- params: float32 [2, 8192, 8192], P(None, ('dp', 'row'), 'col'), may hold values from -4 to 4
- row_factor: float32 [2, 8192], P(None, ('dp', 'row')), may hold values from 0.05 to 500
- col_factor: float32 [2, 8192], P(None, 'col'), may hold values from 0.05 to 500
Outputs:
- new_params: float32 [2, 8192, 8192], P(None, ('dp', 'row'), 'col')
- update: float32 [2, 8192, 8192], P(None, ('dp', 'row'), 'col')
- new_rows: float32 [2, 8192], P(None, ('dp', 'row'))
- new_columns: float32 [2, 8192], P(None, 'col')
The draws below stay inside these ranges and needn't reach their ends.
All inputs are finite; a program needn't handle non-finite values.
Results may differ from the reference program's by a relative error of at most 0.0003.
Values sent between devices are 32-bit elements; how exact they have to be, the bound alone decides.
No kernel may reach another device: no remote copies, remote signals or barrier semaphores. Data moves between devices by JAX's collectives and lax.ppermute only.
A program may use at most 256 MiB of HBM per device.

```python
import math
import jax
import jax.numpy as jnp
from jax import lax

D = 8192
MATS = 2
RB = 1024
N_DP = 4
N_ROW = 2


def factor_levels(key, odd_base, even_base, rise, width):
    odd_matrix = (jnp.arange(MATS) % 2 == 1).reshape(MATS, 1)
    position = (jnp.arange(D, dtype=jnp.float32) / D).reshape(1, D)
    lowest = jnp.where(odd_matrix, math.log(odd_base), math.log(even_base))
    fraction = jax.random.uniform(key, (MATS, D), jnp.float32, 0.0, 1.0)
    return jnp.exp(lowest + position * math.log(rise) + fraction * math.log(width))


def draw_partials(key, part):
    key = jax.random.fold_in(key, 7)
    keys = jax.random.split(key, 4)
    shape = (N_DP, MATS, N_DP, N_ROW, RB, D)
    position = jnp.arange(D, dtype=jnp.float32) / D
    row_scale = jnp.exp(position * math.log(3.0) + jax.random.uniform(keys[0], (D,), jnp.float32, -1.15, 1.15))
    col_scale = jnp.exp(position * math.log(3.0) + jax.random.uniform(keys[1], (D,), jnp.float32, -1.15, 1.15))
    matrix_scale = jnp.where(jnp.arange(MATS) % 2 == 1, 0.08, 1.0).astype(jnp.float32)
    values = 1.5 * jax.random.normal(keys[3], shape, jnp.float32)
    values = values * row_scale.reshape(1, 1, N_DP, N_ROW, RB, 1) * col_scale.reshape(1, 1, 1, 1, 1, D)
    values = values * matrix_scale.reshape(1, MATS, 1, 1, 1, 1)
    return jnp.clip(values, -40.0, 40.0).astype(jnp.bfloat16)


def draw_row_factor(key, part):
    key = jax.random.fold_in(key, 11)
    levels = factor_levels(key, 20.0, 0.05, 10.0, 2.5)
    return jnp.clip(levels, 0.05, 500.0).astype(jnp.float32)


def draw_col_factor(key, part):
    key = jax.random.fold_in(key, 13)
    levels = factor_levels(key, 20.0, 0.05, 10.0, 2.5)
    return jnp.clip(levels, 0.05, 500.0).astype(jnp.float32)


def block_scale(rng, dims, shards, smallest, largest):
    gain = 1.0
    for dim, shards_of in shards:
        draws = jax.random.uniform(jax.random.fold_in(jax.random.fold_in(rng, 6), dim), (shards_of,), jnp.float32, smallest / len(shards), largest / len(shards))
        gain = gain * jnp.repeat(jnp.exp(draws), dims[dim] // shards_of).reshape((-1,) + (1,) * (len(dims) - 1 - dim))
    return gain


def noise(stream_key, extent, scale, most, shards=(), kind=jnp.bfloat16):
    result = jax.random.normal(stream_key, extent, jnp.float32) * scale
    if len(shards) > 0:
        result = block_scale(stream_key, extent, shards, -0.22, 0.18) * result
    return jnp.clip(result, min=-most, max=most).astype(kind)


def setup_inputs(seed: int = 0) -> dict:
    streams_of = jax.random.split(jax.random.key(seed), 5)
    partials = draw_partials(jax.random.fold_in(streams_of[4], 71), 0)
    params = noise(streams_of[1], (MATS, D, D), 0.25, 4.0, ((1, 8), (2, 4)), jnp.float32)
    row_factor = draw_row_factor(jax.random.fold_in(streams_of[4], 71), 0)
    col_factor = draw_col_factor(jax.random.fold_in(streams_of[4], 71), 0)
    return dict(partials=partials, params=params, row_factor=row_factor, col_factor=col_factor)


decay_rate = 1.0 - 2.0 ** (-0.8)
tiny_eps = 1e-30
clip_limit = 1.0
learn_rate = 0.01

def reference(partials, params, row_factor, col_factor):
    params_list = []
    update_list = []
    rows_list = []
    columns_list = []
    for matrix in range(MATS):
        summed = partials[0, matrix].astype(jnp.float32)
        for source in range(1, N_DP):
            summed = summed + partials[source, matrix].astype(jnp.float32)
        summed = summed.reshape(D, D)
        squares = summed * summed
        row_new = decay_rate * row_factor[matrix] + (1.0 - decay_rate) * (lax.optimization_barrier(jnp.sum(squares, axis=1)) / D + tiny_eps)
        col_new = decay_rate * col_factor[matrix] + (1.0 - decay_rate) * (lax.optimization_barrier(jnp.sum(squares, axis=0)) / D + tiny_eps)
        row_level = jnp.sum(row_new) / D
        second = row_new[:, None] * col_new[None, :] / row_level
        scaled = summed * lax.rsqrt(second)
        spread = jnp.sqrt(jnp.sum(scaled * scaled) / (D * D))
        scaled = scaled / jnp.maximum(1.0, spread / clip_limit)
        params_list.append(params[matrix] - learn_rate * scaled)
        update_list.append(scaled)
        rows_list.append(row_new)
        columns_list.append(col_new)
    return (jnp.stack(params_list), jnp.stack(update_list), jnp.stack(rows_list), jnp.stack(columns_list))
```

```python
import jax
import jax.numpy as jnp
from jax import lax
from jax.sharding import PartitionSpec as P

decay_rate = 1.0 - 2.0 ** (-0.8)
tiny_eps = 1e-30
clip_limit = 1.0
learn_rate = 0.01

chunks = 2
in_flight = 2


def swap(x, axes, mask):
    size = lax.axis_size(axes)
    return lax.ppermute(x, axes, [(i, i ^ mask) for i in range(size)])


def exchange_sum(x, axes):
    size = lax.axis_size(axes)
    got = [x] + [swap(x, axes, mask) for mask in range(1, size)]
    while len(got) > 1:
        got = [got[i] + got[i + 1] for i in range(0, len(got), 2)]
    return got[0]


def per_device(partials, params, row_factor, col_factor):
    mats, rows, block_cols = params.shape
    extent = block_cols * lax.axis_size("col")
    me = lax.axis_index("dp")
    part = rows // (2 * chunks)

    def piece(m, mask, start):
        block = lax.dynamic_slice(
            partials,
            (0, m, me ^ mask, 0, start, 0),
            (1, 1, 1, 1, part, block_cols),
        )
        return block.reshape(part, block_cols).astype(jnp.float32)

    sent = {1: [], 2: []}

    def send(x, mask):
        queue = sent[mask]
        if len(queue) >= in_flight:
            x, _ = lax.optimization_barrier((x, queue[-in_flight]))
        queue.append(swap(x, "dp", mask))
        return queue[-1]

    steps = [(m, chunk) for m in range(mats) for chunk in range(chunks)]
    halves = ((1, 2), (2, 1))

    def start_of(chunk, half):
        return (2 * chunk + half) * part

    def send_passed(m, chunk):
        return [send(piece(m, 3, start_of(chunk, h)), first) for h, (first, _) in enumerate(halves)]

    blocks = [[] for _ in range(mats)]
    passed = send_passed(*steps[0])
    for k, (m, chunk) in enumerate(steps):
        if k + 1 < len(steps):
            later = send_passed(*steps[k + 1])
        direct = [send(piece(m, first, start_of(chunk, h)), first) for h, (first, _) in enumerate(halves)]
        hop = [
            send(passed[h] + piece(m, second, start_of(chunk, h)), second)
            for h, (_, second) in enumerate(halves)
        ]
        for h in range(2):
            blocks[m].append(piece(m, 0, start_of(chunk, h)) + direct[h] + hop[h])
        passed = later

    new_params, update, new_rows, new_columns = [], [], [], []
    for m in range(mats):
        summed = jnp.concatenate(blocks[m], axis=0)
        squares = summed * summed
        row_total = exchange_sum(jnp.sum(squares, axis=1), "col")
        col_total = exchange_sum(jnp.sum(squares, axis=0), ("dp", "row"))
        row_new = decay_rate * row_factor[m] + (1.0 - decay_rate) * (row_total / extent + tiny_eps)
        col_new = decay_rate * col_factor[m] + (1.0 - decay_rate) * (col_total / extent + tiny_eps)
        weighted = squares * (1.0 / row_new)[:, None] * (1.0 / col_new)[None, :]
        pair = jnp.stack([jnp.sum(weighted), jnp.sum(row_new)])
        pair = exchange_sum(pair, ("dp", "row"))
        row_level = pair[1] / extent
        total = exchange_sum(pair[0], "col") * row_level
        spread = jnp.sqrt(total / (extent * extent))
        factor = jnp.sqrt(row_level) / jnp.maximum(1.0, spread / clip_limit)
        step = summed * (lax.rsqrt(row_new) * factor)[:, None] * lax.rsqrt(col_new)[None, :]
        new_params.append(params[m] - learn_rate * step)
        update.append(step)
        new_rows.append(row_new)
        new_columns.append(col_new)
    return tuple(jnp.stack(x) for x in (new_params, update, new_rows, new_columns))


def solution(mesh):
    placed = (
        P("dp", None, None, "row", None, "col"),
        P(None, ("dp", "row"), "col"),
        P(None, ("dp", "row")),
        P(None, "col"),
    )
    return jax.shard_map(
        per_device,
        mesh=mesh,
        in_specs=placed,
        out_specs=(
            P(None, ("dp", "row"), "col"),
            P(None, ("dp", "row"), "col"),
            P(None, ("dp", "row")),
            P(None, "col"),
        ),
        check_vma=False,
    )
```

```python
import functools

import jax
import jax.numpy as jnp
from jax import lax
from jax.experimental import pallas as pl
from jax.experimental.pallas import tpu as pltpu
from jax.sharding import PartitionSpec as P

decay_rate = 1.0 - 2.0 ** (-0.8)
tiny_eps = 1e-30
clip_limit = 1.0
learn_rate = 0.01

lanes = 128
sublanes = 8
blocks_of_matrix = 8
tile_rows = 16


def swap(x, axes, mask):
    size = lax.axis_size(axes)
    return lax.ppermute(x, axes, [(i, i ^ mask) for i in range(size)])


def exchange_sum(x, axes):
    size = lax.axis_size(axes)
    got = [x] + [swap(x, axes, mask) for mask in range(1, size)]
    while len(got) > 1:
        got = [got[i] + got[i + 1] for i in range(0, len(got), 2)]
    return got[0]


def pairwise_sum(x, axes):
    mask = 1
    while mask < lax.axis_size(axes):
        x = x + swap(x, axes, mask)
        mask *= 2
    return x


def step_kernel(takes, finishes, sends, starts, *refs):
    refs = list(refs[1:])
    take = lambda yes: refs.pop(0) if yes else None
    got = [take(takes or finishes) for _ in range(2)]
    mine = take(finishes)
    direct = [take(sends) for _ in range(2)]
    relay = [take(sends) for _ in range(2)]
    onward = take(starts)
    cols_in, summed_in, rows_in = take(True), take(finishes), take(finishes)
    out = [take(sends or starts) for _ in range(2)]
    cols_out, summed_out, rows_out = take(True), take(finishes), take(finishes)
    tail_slot = 2 if finishes else 0
    out_slot = 2 if sends else 0

    @pl.when(pl.program_id(0) == 0)
    def _():
        cols_out[...] = cols_in[...]

    f32 = jnp.float32
    for half in range(2):
        if starts:
            out[half][out_slot] = onward[half].astype(f32)
        if sends:
            out[half][0] = direct[half][...].astype(f32)
            out[1 - half][1] = got[half][tail_slot] + relay[half][...].astype(f32)
        if finishes:
            total = mine[half].astype(f32) + got[half][0] + got[1 - half][1]
            summed_out[half] = total
            squares = total * total
            rows_out[half] = sum(
                squares[:, i : i + lanes] for i in range(0, squares.shape[1], lanes)
            )
            cols_out[...] += sum(
                squares[i : i + sublanes] for i in range(0, squares.shape[0], sublanes)
            )


def step(j, total_blocks, me, partials, got, cols, summed, rows):
    mats, _, count, _, part, width = partials.shape
    tile = min(tile_rows, part)
    finishes = j >= 2
    takes = 0 <= j < total_blocks
    sends = takes
    starts = j + 2 < total_blocks
    f32 = jnp.float32

    def piece_spec(block, mask, half):
        m, b = divmod(block, count)
        if half is None:
            return pl.BlockSpec(
                (None, None, None, 2, tile, width),
                lambda t, at: (m, at[0] ^ mask, b, 0, t, 0),
            )
        return pl.BlockSpec(
            (None, None, None, None, tile, width),
            lambda t, at: (m, at[0] ^ mask, b, half, t, 0),
        )

    def message_spec(slots):
        return pl.BlockSpec((slots, tile, width), lambda t, at: (0, t, 0))

    operands, in_specs = [], []

    def add(x, spec):
        operands.append(x)
        in_specs.append(spec)

    if j >= 0:
        for x in got:
            add(x, message_spec(x.shape[0]))
    if finishes:
        add(partials, piece_spec(j - 2, 0, None))
    if sends:
        for half, mask in ((0, 1), (1, 2)):
            add(partials, piece_spec(j, mask, half))
        for half, mask in ((0, 2), (1, 1)):
            add(partials, piece_spec(j, mask, half))
    if starts:
        add(partials, piece_spec(j + 2, 3, None))
    m, b = divmod(max(j - 2, 0), count)
    cols_spec = pl.BlockSpec((None, sublanes, width), lambda t, at: (m, 0, 0))
    done_spec = lambda size: pl.BlockSpec(
        (None, None, 2, tile, size), lambda t, at: (m, b, 0, t, 0)
    )
    add(cols, cols_spec)
    aliases = {len(operands): 2 if sends or starts else 0}
    if finishes:
        for x in (summed, rows):
            add(x, pl.BlockSpec(memory_space=pl.ANY))
            aliases[len(operands)] = max(aliases.values()) + 1

    slots = (2 if sends else 0) + (1 if starts else 0)
    out_shape, out_specs = [], []
    if slots:
        for _ in range(2):
            out_shape.append(jax.ShapeDtypeStruct((slots, part, width), f32))
            out_specs.append(message_spec(slots))
    out_shape.append(jax.ShapeDtypeStruct(cols.shape, f32))
    out_specs.append(cols_spec)
    if finishes:
        for x in (summed, rows):
            out_shape.append(jax.ShapeDtypeStruct(x.shape, f32))
            out_specs.append(done_spec(x.shape[-1]))
    moved = part * width * (4 * (2 * slots + 8) + 2 * 8)
    result = pl.pallas_call(
        functools.partial(step_kernel, takes, finishes, sends, starts),
        out_shape=out_shape,
        grid_spec=pltpu.PrefetchScalarGridSpec(
            num_scalar_prefetch=1,
            grid=(part // tile,),
            in_specs=in_specs,
            out_specs=out_specs,
        ),
        input_output_aliases=aliases,
        compiler_params=pltpu.CompilerParams(vmem_limit_bytes=24 * 1024 * 1024),
        cost_estimate=pl.CostEstimate(
            flops=part * width * 20, bytes_accessed=moved, transcendentals=0
        ),
        name="step",
    )(me, *operands)
    sent = result[:2] if slots else None
    rest = result[2:] if slots else result
    return (sent, rest[0]) + ((rest[1], rest[2]) if finishes else (summed, rows))


def per_device(partials, params, row_factor, col_factor):
    mats, rows, block_cols = params.shape
    extent = block_cols * lax.axis_size("col")
    me = lax.axis_index("dp").astype(jnp.int32).reshape(1)
    count = blocks_of_matrix
    while rows % (2 * count * 16):
        count //= 2
    part = rows // (2 * count)
    total_blocks = mats * count
    pieces = partials.reshape(mats, partials.shape[2], count, 2, part, block_cols)

    cols = jnp.zeros((mats, sublanes, block_cols), jnp.float32)
    summed = jnp.zeros((mats, count, 2, part, block_cols), jnp.float32)
    row_parts = jnp.zeros((mats, count, 2, part, lanes), jnp.float32)
    flying = {}
    for j in range(-2, total_blocks + 2):
        got = flying.pop(j, None)
        sent, cols, summed, row_parts = step(
            j, total_blocks, me, pieces, got, cols, summed, row_parts
        )
        if sent is not None:
            flying[j + 2] = [swap(sent[0], "dp", 1), swap(sent[1], "dp", 2)]

    summed = summed.reshape(params.shape)
    row_total = exchange_sum(jnp.sum(row_parts.reshape(mats, rows, lanes), axis=2), "col")
    row_new = decay_rate * row_factor + (1.0 - decay_rate) * (row_total / extent + tiny_eps)
    weighted = jnp.sum(summed * summed * (1.0 / row_new)[:, :, None], axis=1)
    level = jnp.broadcast_to(jnp.sum(row_new, axis=1)[:, None], (mats, lanes))
    sums = jnp.concatenate([jnp.sum(cols, axis=1), weighted, level], axis=1)
    sums = pairwise_sum(sums, ("dp", "row"))
    col_total, weighted = sums[:, :block_cols], sums[:, block_cols : 2 * block_cols]
    row_level = sums[:, 2 * block_cols] / extent
    col_new = decay_rate * col_factor + (1.0 - decay_rate) * (col_total / extent + tiny_eps)
    total = exchange_sum(jnp.sum(weighted / col_new, axis=1), "col") * row_level
    spread = jnp.sqrt(total / (extent * extent))
    factor = jnp.sqrt(row_level) / jnp.maximum(1.0, spread / clip_limit)
    by_row = lax.rsqrt(row_new) * factor[:, None]
    update = summed * by_row[:, :, None] * lax.rsqrt(col_new)[:, None, :]
    return (params - learn_rate * update, update, row_new, col_new)


def solution(mesh):
    placed = (
        P("dp", None, None, "row", None, "col"),
        P(None, ("dp", "row"), "col"),
        P(None, ("dp", "row")),
        P(None, "col"),
    )
    return jax.shard_map(
        per_device,
        mesh=mesh,
        in_specs=placed,
        out_specs=(
            P(None, ("dp", "row"), "col"),
            P(None, ("dp", "row"), "col"),
            P(None, ("dp", "row")),
            P(None, "col"),
        ),
        check_vma=False,
    )
```

```python
import functools

import jax
import jax.numpy as jnp
from jax import lax
from jax.experimental import pallas as pl
from jax.experimental.pallas import tpu as pltpu
from jax.sharding import PartitionSpec as P

decay_rate = 1.0 - 2.0 ** (-0.8)
tiny_eps = 1e-30
clip_limit = 1.0
learn_rate = 0.01

lanes = 128
sublanes = 8
blocks_of_matrix = 4
tile_rows = 16
finish_rows = 64
f32 = jnp.float32


def swap(x, axes, mask):
    size = lax.axis_size(axes)
    return lax.ppermute(x, axes, [(i, i ^ mask) for i in range(size)])


def exchange_sum(x, axes):
    size = lax.axis_size(axes)
    got = [x] + [swap(x, axes, mask) for mask in range(1, size)]
    while len(got) > 1:
        got = [got[i] + got[i + 1] for i in range(0, len(got), 2)]
    return got[0]


def pairwise_sum(x, axes):
    mask = 1
    while mask < lax.axis_size(axes):
        x = x + swap(x, axes, mask)
        mask *= 2
    return x


def tie(*xs):
    return lax.optimization_barrier(xs)


def params_of(mib):
    return pltpu.CompilerParams(vmem_limit_bytes=mib * 1024 * 1024)


def step_kernel(takes, finishes, first, sends, starts, *refs):
    refs = list(refs[1:])
    take = lambda yes: refs.pop(0) if yes else None
    got = [take(takes or finishes) for _ in range(2)]
    mine = take(finishes)
    direct = [take(sends) for _ in range(2)]
    relay = [take(sends) for _ in range(2)]
    onward = take(starts)
    again = finishes and not first
    cols_in, _, _ = take(again), take(again), take(again)
    out = [take(sends or starts) for _ in range(2)]
    cols_out, summed_out, rows_out = take(finishes), take(finishes), take(finishes)
    row_parts = take(finishes)
    tail_slot = 2 if finishes else 0
    out_slot = 2 if sends else 0
    t = pl.program_id(0)

    if finishes:

        @pl.when(t == 0)
        def _():
            cols_out[...] = jnp.zeros_like(cols_out) if first else cols_in[...]

    for half in range(2):
        if starts:
            out[half][out_slot] = onward[half].astype(f32)
        if sends:
            out[half][0] = direct[half][...].astype(f32)
            out[1 - half][1] = got[half][tail_slot] + relay[half][...].astype(f32)
        if finishes:
            total = mine[half].astype(f32) + got[half][0] + got[1 - half][1]
            summed_out[half] = total
            squares = total * total
            tile, width = squares.shape
            part = row_parts.shape[0] // 2
            row_parts[pl.ds(pl.multiple_of(half * part + t * tile, sublanes), tile)] = sum(
                squares[:, i : i + lanes] for i in range(0, width, lanes)
            )
            cols_out[...] += sum(squares[i : i + sublanes] for i in range(0, tile, sublanes))

    if finishes:

        @pl.when(t == pl.num_programs(0) - 1)
        def _():
            rows_out[...] = lax.dot_general(
                jnp.ones((sublanes, lanes), f32),
                row_parts[...],
                (((1,), (1,)), ((), ())),
                precision=lax.Precision.HIGHEST,
                preferred_element_type=f32,
            )


def step(j, total_blocks, me, partials, got, sums):
    mats, _, count, _, part, width = partials.shape
    tile = min(tile_rows, part)
    finishes = j >= 2
    takes = 0 <= j < total_blocks
    sends = takes
    starts = j + 2 < total_blocks
    b = (j - 2) % count
    first = finishes and b == 0

    def piece_spec(block, mask, half):
        m, b = divmod(block, count)
        if half is None:
            return pl.BlockSpec(
                (None, None, None, 2, tile, width),
                lambda t, at: (m, at[0] ^ mask, b, 0, t, 0),
            )
        return pl.BlockSpec(
            (None, None, None, None, tile, width),
            lambda t, at: (m, at[0] ^ mask, b, half, t, 0),
        )

    def message_spec(slots):
        return pl.BlockSpec((slots, tile, width), lambda t, at: (0, t, 0))

    operands, in_specs = [], []

    def add(x, spec):
        operands.append(x)
        in_specs.append(spec)

    if j >= 0:
        for x in got:
            add(x, message_spec(x.shape[0]))
    if finishes:
        add(partials, piece_spec(j - 2, 0, None))
    if sends:
        for half, mask in ((0, 1), (1, 2)):
            add(partials, piece_spec(j, mask, half))
        for half, mask in ((0, 2), (1, 1)):
            add(partials, piece_spec(j, mask, half))
    if starts:
        add(partials, piece_spec(j + 2, 3, None))

    slots = (2 if sends else 0) + (1 if starts else 0)
    out_shape, out_specs, scratch, aliases = [], [], [], {}
    if slots:
        for _ in range(2):
            out_shape.append(jax.ShapeDtypeStruct((slots, part, width), f32))
            out_specs.append(message_spec(slots))
    if finishes:
        cols_spec = pl.BlockSpec((sublanes, width), lambda t, at: (0, 0))
        if not first:
            add(sums[0], cols_spec)
            for i in (1, 2):
                aliases[1 + len(operands)] = len(out_shape) + i
                add(sums[i], pl.BlockSpec(memory_space=pl.ANY))
        out_shape.append(jax.ShapeDtypeStruct((sublanes, width), f32))
        out_specs.append(cols_spec)
        out_shape.append(jax.ShapeDtypeStruct((count, 2, part, width), f32))
        out_specs.append(pl.BlockSpec((None, 2, tile, width), lambda t, at: (b, 0, t, 0)))
        out_shape.append(jax.ShapeDtypeStruct((count, sublanes, 2 * part), f32))
        out_specs.append(pl.BlockSpec((None, sublanes, 2 * part), lambda t, at: (b, 0, 0)))
        scratch.append(pltpu.VMEM((2 * part, lanes), f32))
    moved = part * width * (4 * (2 * slots + 8) + 2 * 8)
    result = pl.pallas_call(
        functools.partial(step_kernel, takes, finishes, first, sends, starts),
        out_shape=out_shape,
        grid_spec=pltpu.PrefetchScalarGridSpec(
            num_scalar_prefetch=1,
            grid=(part // tile,),
            in_specs=in_specs,
            out_specs=out_specs,
            scratch_shapes=scratch,
        ),
        input_output_aliases=aliases,
        compiler_params=params_of(24),
        cost_estimate=pl.CostEstimate(
            flops=part * width * 20, bytes_accessed=moved, transcendentals=0
        ),
        name="step",
    )(me, *operands)
    sent = result[:2] if slots else None
    return sent, tuple(result[2:] if slots else result) if finishes else None


def weighted_kernel(extent, totals, factor, cols, summed, rows_out, stats, weighted, level):
    i = pl.program_id(0)

    @pl.when(i == 0)
    def _():
        weighted[...] = jnp.zeros_like(weighted)
        level[...] = jnp.zeros_like(level)

    row_new = decay_rate * factor[...] + (1.0 - decay_rate) * (totals[...] / extent + tiny_eps)
    rows_out[...] = row_new
    level[...] += row_new
    inverse = jnp.transpose(1.0 / row_new)[:, 0:1]
    part = summed.shape[1]
    for half in range(2):
        for r in range(0, part, sublanes):
            x = summed[half, r : r + sublanes]
            at = half * part + r
            weighted[...] += x * x * inverse[at : at + sublanes]

    @pl.when(i == pl.num_programs(0) - 1)
    def _():
        stats[...] = jnp.zeros_like(stats)
        stats[0:1] = jnp.sum(cols[...], axis=0, keepdims=True)
        stats[1:2] = jnp.sum(weighted[...], axis=0, keepdims=True)
        total = jnp.sum(level[0:1], axis=1, keepdims=True)
        stats[2:3] = jnp.broadcast_to(total, (1, stats.shape[1]))


def weighted_sums(extent, totals, factor, cols, summed):
    count, _, part, width = summed.shape
    along = pl.BlockSpec((None, sublanes, 2 * part), lambda i: (i, 0, 0))
    whole = pl.BlockSpec((sublanes, width), lambda i: (0, 0))
    return pl.pallas_call(
        functools.partial(weighted_kernel, extent),
        grid=(count,),
        in_specs=[
            along,
            pl.BlockSpec((None, 1, 2 * part), lambda i: (i, 0, 0)),
            whole,
            pl.BlockSpec((None, 2, part, width), lambda i: (i, 0, 0, 0)),
        ],
        out_specs=[along, whole],
        out_shape=[
            jax.ShapeDtypeStruct(totals.shape, f32),
            jax.ShapeDtypeStruct((sublanes, width), f32),
        ],
        scratch_shapes=[pltpu.VMEM((sublanes, width), f32), pltpu.VMEM((sublanes, 2 * part), f32)],
        compiler_params=params_of(16),
        cost_estimate=pl.CostEstimate(
            flops=3 * summed.size, bytes_accessed=4 * summed.size, transcendentals=0
        ),
        name="weighted",
    )(totals, factor.reshape(count, 1, 2 * part), cols, summed)


def finish_kernel(m, tile, by_row, by_col, summed, params, *refs):
    new_params, update, column = refs[-3:]
    count, _, part, width = summed.shape
    for i in range(count):
        column[i] = jnp.transpose(by_row[i])

    def body(x, p, new_p, moved):
        i, half, t = (pl.program_id(axis) for axis in range(3))
        start = pl.multiple_of(half * part + t * tile, sublanes)
        y = x[...] * column[i, pl.ds(start, tile)][:, 0:1] * by_col[...]
        moved[...] = y
        new_p[...] = p[...] - learn_rate * y

    of_sum = pl.BlockSpec((None, None, tile, width), lambda i, h, t: (i, h, t, 0))
    of_matrix = pl.BlockSpec((None, None, None, tile, width), lambda i, h, t: (m, i, h, t, 0))
    pltpu.emit_pipeline(
        body,
        grid=(count, 2, part // tile),
        in_specs=[of_sum, of_matrix],
        out_specs=[of_matrix] * 2,
    )(summed, params, new_params, update)


def finish(m, by_row, by_col, summed, params, outs):
    count, _, part, width = summed.shape
    held = () if outs is None else outs
    in_hbm = pl.BlockSpec(memory_space=pltpu.HBM)
    return pl.pallas_call(
        functools.partial(finish_kernel, m, min(part, finish_rows)),
        in_specs=[
            pl.BlockSpec(memory_space=pltpu.VMEM),
            pl.BlockSpec(memory_space=pltpu.VMEM),
            pl.BlockSpec(memory_space=pl.ANY),
            in_hbm,
        ]
        + [in_hbm] * len(held),
        out_specs=[in_hbm] * 2,
        out_shape=[jax.ShapeDtypeStruct(params.shape, f32)] * 2,
        scratch_shapes=[pltpu.VMEM((count, 2 * part, sublanes), f32)],
        input_output_aliases={4 + i: i for i in range(len(held))},
        compiler_params=params_of(44),
        cost_estimate=pl.CostEstimate(
            flops=4 * summed.size, bytes_accessed=16 * summed.size, transcendentals=0
        ),
        name="finish",
    )(by_row, by_col, summed, params, *held)


def per_device(partials, params, row_factor, col_factor):
    mats, rows, block_cols = params.shape
    extent = block_cols * lax.axis_size("col")
    me = lax.axis_index("dp").astype(jnp.int32).reshape(1)
    count = blocks_of_matrix
    part = rows // (2 * count)
    total_blocks = mats * count
    pieces = partials.reshape(mats, partials.shape[2], count, 2, part, block_cols)
    blocked = params.reshape(mats, count, 2, part, block_cols)

    new_rows, new_columns = [], []

    def row_stage(m, sums):
        cols, summed, rows_along = sums
        totals = exchange_sum(rows_along, "col")
        row_new, stats = weighted_sums(extent, totals, row_factor[m], cols, summed)
        new_rows.append(row_new[:, 0].reshape(rows))
        return row_new, stats

    def col_stage(m, stats):
        col_new = decay_rate * col_factor[m : m + 1] + (1.0 - decay_rate) * (
            stats[0:1] / extent + tiny_eps
        )
        new_columns.append(col_new)
        return col_new, stats[2, 0] / extent, jnp.sum(stats[1:2] / col_new)

    def last_stage(row_new, col_new, row_level, total):
        spread = jnp.sqrt(total * row_level / (extent * extent))
        factor = jnp.sqrt(row_level) / jnp.maximum(1.0, spread / clip_limit)
        return lax.rsqrt(row_new) * factor, lax.rsqrt(col_new)

    flying = {}
    sums = None
    row_news, stats, summeds = [], [], []
    for j in range(-2, total_blocks + 2):
        m, b = divmod(j - 2, count)
        got = flying.pop(j, None)
        sent, sums = step(j, total_blocks, me, pieces, got, sums)
        if sums:
            me, *sums = tie(me, *sums)
        else:
            me, *sent = tie(me, *sent)
        if sent is not None:
            flying[j + 2] = [swap(sent[0], "dp", 1), swap(sent[1], "dp", 2)]
        if 0 <= m < mats - 1 and b == count - 1:
            row_new, own = row_stage(m, sums)
            me, own = tie(me, pairwise_sum(own, "row"))
            row_news.append(row_new)
            stats.append(own)
            summeds.append(sums[1])
        if j == total_blocks:
            earlier = [exchange_sum(own, "dp") for own in tie(*stats, me)[:-1]]

    ready = []
    for m, own in enumerate(earlier):
        own, *sums = tie(own, *sums)
        col_new, row_level, total = col_stage(m, own)
        ready.append((row_news[m], col_new, row_level, exchange_sum(total, "col")))
    row_new, own = row_stage(mats - 1, sums)
    own = pairwise_sum(own, "row")
    outs = None
    for m, values in enumerate(ready):
        own, *values = tie(own, *values)
        outs = finish(m, *last_stage(*values), summeds[m], blocked, outs)
    own = exchange_sum(own, "dp")
    col_new, row_level, total = col_stage(mats - 1, own)
    if outs is not None:
        total, *outs = tie(total, *outs)
    by_row, by_col = last_stage(row_new, col_new, row_level, exchange_sum(total, "col"))
    new_params, update = finish(mats - 1, by_row, by_col, sums[1], blocked, outs)
    return (
        new_params.reshape(params.shape),
        update.reshape(params.shape),
        jnp.stack(new_rows),
        jnp.concatenate(new_columns, axis=0),
    )


def solution(mesh):
    placed = (
        P("dp", None, None, "row", None, "col"),
        P(None, ("dp", "row"), "col"),
        P(None, ("dp", "row")),
        P(None, "col"),
    )
    return jax.shard_map(
        per_device,
        mesh=mesh,
        in_specs=placed,
        out_specs=(
            P(None, ("dp", "row"), "col"),
            P(None, ("dp", "row"), "col"),
            P(None, ("dp", "row")),
            P(None, "col"),
        ),
        check_vma=False,
    )
```

```python
import functools

import jax
import jax.numpy as jnp
from jax import lax
from jax.experimental import pallas as pl
from jax.experimental.pallas import tpu as pltpu
from jax.sharding import PartitionSpec as P

decay_rate = 1.0 - 2.0 ** (-0.8)
tiny_eps = 1e-30
clip_limit = 1.0
learn_rate = 0.01

lanes = 128
sublanes = 8
blocks_of_matrix = 8
tile_rows = 16
finish_rows = 64
f32 = jnp.float32


def swap(x, axes, mask):
    size = lax.axis_size(axes)
    return lax.ppermute(x, axes, [(i, i ^ mask) for i in range(size)])


def exchange(x, axes):
    return [x] + [swap(x, axes, mask) for mask in range(1, lax.axis_size(axes))]


def tree_sum(got):
    while len(got) > 1:
        got = [got[i] + got[i + 1] for i in range(0, len(got), 2)]
    return got[0]


def pairwise_sum(x, axes):
    mask = 1
    while mask < lax.axis_size(axes):
        x = x + swap(x, axes, mask)
        mask *= 2
    return x


def tie(*xs):
    return lax.optimization_barrier(xs)


def params_of(mib):
    return pltpu.CompilerParams(vmem_limit_bytes=mib * 1024 * 1024)


def step_kernel(takes, finishes, first, sends, starts, brings, carries, *refs):
    refs = list(refs[1:])
    take = lambda yes: refs.pop(0) if yes else None
    got = [take(takes or finishes) for _ in range(2)]
    mine = take(finishes)
    direct = [take(sends) for _ in range(2)]
    relay = [take(sends) for _ in range(2)]
    onward = take(starts)
    again = finishes and not first
    cols_in, _, _ = take(again), take(again), take(again)
    stats_in = take(brings is not None or carries is not None)
    out = [take(sends or starts) for _ in range(2)]
    cols_out, summed_out, rows_out = take(finishes), take(finishes), take(finishes)
    stats_out = take(brings is not None)
    row_parts = take(finishes)
    t = pl.program_id(0)
    tile, width = (onward if starts else mine if finishes else direct[0]).shape[-2:]
    part = tile * pl.num_programs(0)

    def rows_of(slot):
        return pl.ds(pl.multiple_of(slot * part + t * tile, sublanes), tile)

    @pl.when(t == 0)
    def _():
        if finishes:
            cols_out[...] = jnp.zeros_like(cols_out) if first else cols_in[...]
        if brings is not None:
            stats_out[...] = stats_in[...] + got[brings][got[brings].shape[0] - sublanes :]
        if carries is not None:
            stats = stats_in if brings is None else stats_out
            out[carries][out[carries].shape[0] - sublanes :] = stats[...]

    for half in range(2):
        if starts:
            out[half][rows_of(2 if sends else 0)] = onward[half].astype(f32)
        if sends:
            out[half][rows_of(0)] = direct[half][...].astype(f32)
            passed = got[half][rows_of(2 if finishes else 0)]
            out[1 - half][rows_of(1)] = passed + relay[half][...].astype(f32)
        if finishes:
            total = mine[half].astype(f32) + got[half][rows_of(0)] + got[1 - half][rows_of(1)]
            summed_out[half] = total
            squares = total * total
            row_parts[rows_of(half)] = sum(squares[:, i : i + lanes] for i in range(0, width, lanes))
            cols_out[...] += sum(squares[i : i + sublanes] for i in range(0, tile, sublanes))

    if finishes:

        @pl.when(t == pl.num_programs(0) - 1)
        def _():
            rows_out[...] = lax.dot_general(
                jnp.ones((sublanes, lanes), f32),
                row_parts[...],
                (((1,), (1,)), ((), ())),
                precision=lax.Precision.HIGHEST,
                preferred_element_type=f32,
            )


def step(j, total_blocks, me, partials, got, sums, stats, brings, carries):
    mats, _, count, _, part, width = partials.shape
    tile = min(tile_rows, part)
    finishes = j >= 2
    takes = 0 <= j < total_blocks
    sends = takes
    starts = j + 2 < total_blocks
    b = (j - 2) % count
    first = finishes and b == 0

    def piece_spec(block, mask, half):
        m, b = divmod(block, count)
        if half is None:
            return pl.BlockSpec(
                (None, None, None, 2, tile, width),
                lambda t, at: (m, at[0] ^ mask, b, 0, t, 0),
            )
        return pl.BlockSpec(
            (None, None, None, None, tile, width),
            lambda t, at: (m, at[0] ^ mask, b, half, t, 0),
        )

    in_vmem = pl.BlockSpec(memory_space=pltpu.VMEM)
    operands, in_specs = [], []

    def add(x, spec):
        operands.append(x)
        in_specs.append(spec)

    if j >= 0:
        for x in got:
            add(x, in_vmem)
    if finishes:
        add(partials, piece_spec(j - 2, 0, None))
    if sends:
        for half, mask in ((0, 1), (1, 2)):
            add(partials, piece_spec(j, mask, half))
        for half, mask in ((0, 2), (1, 1)):
            add(partials, piece_spec(j, mask, half))
    if starts:
        add(partials, piece_spec(j + 2, 3, None))

    slots = (2 if sends else 0) + (1 if starts else 0)
    out_shape, out_specs, scratch, aliases = [], [], [], {}
    if slots:
        for link in range(2):
            size = slots * part + (sublanes if link == carries else 0)
            out_shape.append(jax.ShapeDtypeStruct((size, width), f32))
            out_specs.append(in_vmem)
    cols_spec = pl.BlockSpec((sublanes, width), lambda t, at: (0, 0))
    if finishes:
        if not first:
            add(sums[0], cols_spec)
            for i in (1, 2):
                aliases[1 + len(operands)] = len(out_shape) + i
                add(sums[i], pl.BlockSpec(memory_space=pl.ANY))
        out_shape.append(jax.ShapeDtypeStruct((sublanes, width), f32))
        out_specs.append(cols_spec)
        out_shape.append(jax.ShapeDtypeStruct((count, 2, part, width), f32))
        out_specs.append(pl.BlockSpec((None, 2, tile, width), lambda t, at: (b, 0, t, 0)))
        out_shape.append(jax.ShapeDtypeStruct((count, sublanes, 2 * part), f32))
        out_specs.append(pl.BlockSpec((None, sublanes, 2 * part), lambda t, at: (b, 0, 0)))
        scratch.append(pltpu.VMEM((2 * part, lanes), f32))
    if brings is not None or carries is not None:
        add(stats, cols_spec)
    if brings is not None:
        out_shape.append(jax.ShapeDtypeStruct((sublanes, width), f32))
        out_specs.append(cols_spec)
    moved = part * width * (4 * (2 * slots + 8) + 2 * 8)
    result = pl.pallas_call(
        functools.partial(step_kernel, takes, finishes, first, sends, starts, brings, carries),
        out_shape=out_shape,
        grid_spec=pltpu.PrefetchScalarGridSpec(
            num_scalar_prefetch=1,
            grid=(part // tile,),
            in_specs=in_specs,
            out_specs=out_specs,
            scratch_shapes=scratch,
        ),
        input_output_aliases=aliases,
        compiler_params=params_of(34),
        cost_estimate=pl.CostEstimate(
            flops=part * width * 20, bytes_accessed=moved, transcendentals=0
        ),
        name="step",
    )(me, *operands)
    sent = list(result[:2]) if slots else None
    rest = list(result[2:] if slots else result)
    return sent, rest[:3] if finishes else None, rest[3] if brings is not None else stats


def weighted_kernel(extent, factor, cols, summed, *refs):
    *totals, rows_out, stats, weighted, level = refs
    i = pl.program_id(0)

    @pl.when(i == 0)
    def _():
        weighted[...] = jnp.zeros_like(weighted)
        level[...] = jnp.zeros_like(level)

    total = tree_sum([x[...] for x in totals])
    row_new = decay_rate * factor[...] + (1.0 - decay_rate) * (total / extent + tiny_eps)
    rows_out[...] = row_new
    level[...] += row_new
    inverse = jnp.transpose(1.0 / row_new)[:, 0:1]
    part = summed.shape[1]
    for half in range(2):
        for r in range(0, part, sublanes):
            x = summed[half, r : r + sublanes]
            at = half * part + r
            weighted[...] += x * x * inverse[at : at + sublanes]

    @pl.when(i == pl.num_programs(0) - 1)
    def _():
        stats[...] = jnp.zeros_like(stats)
        stats[0:1] = jnp.sum(cols[...], axis=0, keepdims=True)
        stats[1:2] = jnp.sum(weighted[...], axis=0, keepdims=True)
        total = jnp.sum(level[0:1], axis=1, keepdims=True)
        stats[2:3] = jnp.broadcast_to(total, (1, stats.shape[1]))


def weighted_sums(extent, totals, factor, cols, summed):
    count, _, part, width = summed.shape
    along = pl.BlockSpec((None, sublanes, 2 * part), lambda i: (i, 0, 0))
    whole = pl.BlockSpec((sublanes, width), lambda i: (0, 0))
    return pl.pallas_call(
        functools.partial(weighted_kernel, extent),
        grid=(count,),
        in_specs=[
            pl.BlockSpec((None, 1, 2 * part), lambda i: (i, 0, 0)),
            whole,
            pl.BlockSpec((None, 2, part, width), lambda i: (i, 0, 0, 0)),
        ]
        + [along] * len(totals),
        out_specs=[along, whole],
        out_shape=[
            jax.ShapeDtypeStruct(totals[0].shape, f32),
            jax.ShapeDtypeStruct((sublanes, width), f32),
        ],
        scratch_shapes=[pltpu.VMEM((sublanes, width), f32), pltpu.VMEM((sublanes, 2 * part), f32)],
        compiler_params=params_of(16),
        cost_estimate=pl.CostEstimate(
            flops=3 * summed.size, bytes_accessed=4 * summed.size, transcendentals=0
        ),
        name="weighted",
    )(factor.reshape(count, 1, 2 * part), cols, summed, *totals)


def column_kernel(extent, factor, *refs):
    *parts, cols_out, pair = refs
    stats = tree_sum([x[...] for x in parts])
    col_new = decay_rate * factor[...] + (1.0 - decay_rate) * (stats[0:1] / extent + tiny_eps)
    cols_out[...] = col_new
    total = jnp.sum(stats[1:2] / col_new, axis=1, keepdims=True)
    pair[...] = jnp.zeros_like(pair)
    pair[0:1] = jnp.broadcast_to(total, (1, lanes))
    pair[1:2] = stats[2:3, :lanes] / extent


def column_stage(extent, factor, parts):
    return pl.pallas_call(
        functools.partial(column_kernel, extent),
        in_specs=[pl.BlockSpec(memory_space=pltpu.VMEM)] * (1 + len(parts)),
        out_specs=[pl.BlockSpec(memory_space=pltpu.VMEM)] * 2,
        out_shape=[
            jax.ShapeDtypeStruct(factor.shape, f32),
            jax.ShapeDtypeStruct((sublanes, lanes), f32),
        ],
        name="column",
    )(factor, *parts)


def finish_kernel(m, tile, extent, partners, row_new, col_new, summed, params, *refs):
    pairs, (new_params, update, column, by_col) = refs[:partners], refs[-4:]
    count, _, part, width = summed.shape
    row_level = pairs[0][1:2, 0:1]
    total = tree_sum([x[0:1, 0:1] for x in pairs]) * row_level
    spread = jnp.sqrt(total / (extent * extent))
    factor = jnp.sqrt(row_level) / jnp.maximum(1.0, spread / clip_limit)
    by_col[...] = lax.rsqrt(col_new[...])
    for i in range(count):
        column[i] = jnp.transpose(lax.rsqrt(row_new[i]) * factor)

    def body(x, p, new_p, moved):
        i, half, t = (pl.program_id(axis) for axis in range(3))
        start = pl.multiple_of(half * part + t * tile, sublanes)
        y = x[...] * column[i, pl.ds(start, tile)][:, 0:1] * by_col[...]
        moved[...] = y
        new_p[...] = p[...] - learn_rate * y

    of_sum = pl.BlockSpec((None, None, tile, width), lambda i, h, t: (i, h, t, 0))
    of_matrix = pl.BlockSpec((None, None, None, tile, width), lambda i, h, t: (m, i, h, t, 0))
    pltpu.emit_pipeline(
        body,
        grid=(count, 2, part // tile),
        in_specs=[of_sum, of_matrix],
        out_specs=[of_matrix] * 2,
    )(summed, params, new_params, update)


def finish(m, extent, row_new, col_new, pairs, summed, params, outs, mib):
    count, _, part, width = summed.shape
    held = () if outs is None else outs
    in_hbm = pl.BlockSpec(memory_space=pltpu.HBM)
    in_vmem = pl.BlockSpec(memory_space=pltpu.VMEM)
    return pl.pallas_call(
        functools.partial(finish_kernel, m, min(part, finish_rows), extent, len(pairs)),
        in_specs=[in_vmem, in_vmem, pl.BlockSpec(memory_space=pl.ANY), in_hbm]
        + [in_vmem] * len(pairs)
        + [in_hbm] * len(held),
        out_specs=[in_hbm] * 2,
        out_shape=[jax.ShapeDtypeStruct(params.shape, f32)] * 2,
        scratch_shapes=[
            pltpu.VMEM((count, 2 * part, sublanes), f32),
            pltpu.VMEM((1, width), f32),
        ],
        input_output_aliases={4 + len(pairs) + i: i for i in range(len(held))},
        compiler_params=params_of(mib),
        cost_estimate=pl.CostEstimate(
            flops=4 * summed.size, bytes_accessed=16 * summed.size, transcendentals=0
        ),
        name="finish",
    )(row_new, col_new, summed, params, *pairs, *held)


def per_device(partials, params, row_factor, col_factor):
    mats, rows, block_cols = params.shape
    extent = block_cols * lax.axis_size("col")
    me = lax.axis_index("dp").astype(jnp.int32).reshape(1)
    count = blocks_of_matrix
    part = rows // (2 * count)
    total_blocks = mats * count
    pieces = partials.reshape(mats, partials.shape[2], count, 2, part, block_cols)
    blocked = params.reshape(mats, count, 2, part, block_cols)
    new_rows, new_columns = [], []

    def row_stage(m, sums):
        cols, summed, rows_along = sums
        row_new, stats = weighted_sums(
            extent, exchange(rows_along, "col"), row_factor[m], cols, summed
        )
        new_rows.append(row_new[:, 0].reshape(rows))
        return row_new, pairwise_sum(stats, "row")

    def col_stage(m, parts):
        col_new, pair = column_stage(extent, col_factor[m : m + 1], parts)
        new_columns.append(col_new)
        return col_new, exchange(pair, "col")

    flying = {}
    sums = stats = outs = None
    last = {}
    for j in range(-2, total_blocks + 2):
        m, b = divmod(j - 2, count)
        since = b + 1 if m >= 1 else None
        carries = {1: 0, 3: 1}.get(since)
        brings = {3: 0, 5: 1}.get(since)
        got = flying.pop(j, None)
        sent, sums, stats = step(
            j, total_blocks, me, pieces, got, sums, stats, brings, carries
        )
        if sent is not None:
            flying[j + 2] = [swap(sent[0], "dp", 1), swap(sent[1], "dp", 2)]
        if sums:
            me, *sums = tie(me, *sums)
        else:
            me, *_ = tie(me, *sent)
        if 0 <= m < mats - 1 and b == count - 1:
            row_new, stats = row_stage(m, sums)
            last = dict(m=m, row_new=row_new, summed=sums[1])
            me, stats = tie(me, stats)
        if since == 5:
            stats, me = tie(stats, me)
            col_new, pairs = col_stage(last["m"], [stats])
            outs = finish(
                last["m"], extent, last["row_new"], col_new, pairs, last["summed"], blocked, outs, 36
            )
            me, *outs = tie(me, *outs)

    row_new, stats = row_stage(mats - 1, sums)
    col_new, pairs = col_stage(mats - 1, exchange(stats, "dp"))
    new_params, update = finish(
        mats - 1, extent, row_new, col_new, pairs, sums[1], blocked, outs, 44
    )
    return (
        new_params.reshape(params.shape),
        update.reshape(params.shape),
        jnp.stack(new_rows),
        jnp.concatenate(new_columns, axis=0),
    )


def solution(mesh):
    placed = (
        P("dp", None, None, "row", None, "col"),
        P(None, ("dp", "row"), "col"),
        P(None, ("dp", "row")),
        P(None, "col"),
    )
    return jax.shard_map(
        per_device,
        mesh=mesh,
        in_specs=placed,
        out_specs=(
            P(None, ("dp", "row"), "col"),
            P(None, ("dp", "row"), "col"),
            P(None, ("dp", "row")),
            P(None, "col"),
        ),
        check_vma=False,
    )
```

```python
import functools

import jax
import jax.numpy as jnp
from jax import lax
from jax.experimental import pallas as pl
from jax.experimental.pallas import tpu as pltpu
from jax.sharding import PartitionSpec as P

decay_rate = 1.0 - 2.0 ** (-0.8)
tiny_eps = 1e-30
clip_limit = 1.0
learn_rate = 0.01

lanes = 128
sublanes = 8
blocks_of_matrix = 8
tile_rows = 16
f32 = jnp.float32


def swap(x, axes, mask):
    size = lax.axis_size(axes)
    return lax.ppermute(x, axes, [(i, i ^ mask) for i in range(size)])


def exchange(x, axes):
    return [x] + [swap(x, axes, mask) for mask in range(1, lax.axis_size(axes))]


def tree_sum(got):
    while len(got) > 1:
        got = [got[i] + got[i + 1] for i in range(0, len(got), 2)]
    return got[0]


def pairwise_sum(x, axes):
    mask = 1
    while mask < lax.axis_size(axes):
        x = x + swap(x, axes, mask)
        mask *= 2
    return x


def tie(*xs):
    return lax.optimization_barrier(xs)


def params_of(mib):
    return pltpu.CompilerParams(vmem_limit_bytes=mib * 1024 * 1024)


def step_kernel(takes, finishes, first, sends, starts, brings, carries, *refs):
    refs = list(refs[1:])
    take = lambda yes: refs.pop(0) if yes else None
    got = [take(takes or finishes) for _ in range(2)]
    mine = take(finishes)
    direct = [take(sends) for _ in range(2)]
    relay = [take(sends) for _ in range(2)]
    onward = take(starts)
    again = finishes and not first
    cols_in, _, _ = take(again), take(again), take(again)
    stats_in = take(brings is not None or carries is not None)
    out = [take(sends or starts) for _ in range(2)]
    cols_out, summed_out, rows_out = take(finishes), take(finishes), take(finishes)
    stats_out = take(brings is not None)
    row_parts = take(finishes)
    t = pl.program_id(0)
    tile, width = (onward if starts else mine if finishes else direct[0]).shape[-2:]
    part = tile * pl.num_programs(0)

    def rows_of(slot):
        return pl.ds(pl.multiple_of(slot * part + t * tile, sublanes), tile)

    @pl.when(t == 0)
    def _():
        if finishes:
            cols_out[...] = jnp.zeros_like(cols_out) if first else cols_in[...]
        if brings is not None:
            stats_out[...] = stats_in[...] + got[brings][got[brings].shape[0] - sublanes :]
        if carries is not None:
            stats = stats_in if brings is None else stats_out
            out[carries][out[carries].shape[0] - sublanes :] = stats[...]

    for half in range(2):
        if starts:
            out[half][rows_of(2 if sends else 0)] = onward[half].astype(f32)
        if sends:
            out[half][rows_of(0)] = direct[half][...].astype(f32)
            passed = got[half][rows_of(2 if finishes else 0)]
            out[1 - half][rows_of(1)] = passed + relay[half][...].astype(f32)
        if finishes:
            total = mine[half].astype(f32) + got[half][rows_of(0)] + got[1 - half][rows_of(1)]
            summed_out[half] = total
            squares = total * total
            row_parts[rows_of(half)] = sum(squares[:, i : i + lanes] for i in range(0, width, lanes))
            cols_out[...] += sum(squares[i : i + sublanes] for i in range(0, tile, sublanes))

    if finishes:

        @pl.when(t == pl.num_programs(0) - 1)
        def _():
            rows_out[...] = lax.dot_general(
                jnp.ones((sublanes, lanes), f32),
                row_parts[...],
                (((1,), (1,)), ((), ())),
                precision=lax.Precision.HIGHEST,
                preferred_element_type=f32,
            )


def step(j, total_blocks, me, partials, got, sums, stats, brings, carries):
    mats, _, count, _, part, width = partials.shape
    tile = min(tile_rows, part)
    finishes = j >= 2
    takes = 0 <= j < total_blocks
    sends = takes
    starts = j + 2 < total_blocks
    b = (j - 2) % count
    first = finishes and b == 0

    def piece_spec(block, mask, half):
        m, b = divmod(block, count)
        if half is None:
            return pl.BlockSpec(
                (None, None, None, 2, tile, width),
                lambda t, at: (m, at[0] ^ mask, b, 0, t, 0),
            )
        return pl.BlockSpec(
            (None, None, None, None, tile, width),
            lambda t, at: (m, at[0] ^ mask, b, half, t, 0),
        )

    in_vmem = pl.BlockSpec(memory_space=pltpu.VMEM)
    operands, in_specs = [], []

    def add(x, spec):
        operands.append(x)
        in_specs.append(spec)

    if j >= 0:
        for x in got:
            add(x, in_vmem)
    if finishes:
        add(partials, piece_spec(j - 2, 0, None))
    if sends:
        for half, mask in ((0, 1), (1, 2)):
            add(partials, piece_spec(j, mask, half))
        for half, mask in ((0, 2), (1, 1)):
            add(partials, piece_spec(j, mask, half))
    if starts:
        add(partials, piece_spec(j + 2, 3, None))

    slots = (2 if sends else 0) + (1 if starts else 0)
    out_shape, out_specs, scratch, aliases = [], [], [], {}
    if slots:
        for link in range(2):
            size = slots * part + (sublanes if link == carries else 0)
            out_shape.append(jax.ShapeDtypeStruct((size, width), f32))
            out_specs.append(in_vmem)
    cols_spec = pl.BlockSpec((sublanes, width), lambda t, at: (0, 0))
    if finishes:
        if not first:
            add(sums[0], cols_spec)
            for i in (1, 2):
                aliases[1 + len(operands)] = len(out_shape) + i
                add(sums[i], pl.BlockSpec(memory_space=pl.ANY))
        out_shape.append(jax.ShapeDtypeStruct((sublanes, width), f32))
        out_specs.append(cols_spec)
        out_shape.append(jax.ShapeDtypeStruct((count, 2, part, width), f32))
        out_specs.append(pl.BlockSpec((None, 2, tile, width), lambda t, at: (b, 0, t, 0)))
        out_shape.append(jax.ShapeDtypeStruct((count, sublanes, 2 * part), f32))
        out_specs.append(pl.BlockSpec((None, sublanes, 2 * part), lambda t, at: (b, 0, 0)))
        scratch.append(pltpu.VMEM((2 * part, lanes), f32))
    if brings is not None or carries is not None:
        add(stats, cols_spec)
    if brings is not None:
        out_shape.append(jax.ShapeDtypeStruct((sublanes, width), f32))
        out_specs.append(cols_spec)
    moved = part * width * (4 * (2 * slots + 8) + 2 * 8)
    result = pl.pallas_call(
        functools.partial(step_kernel, takes, finishes, first, sends, starts, brings, carries),
        out_shape=out_shape,
        grid_spec=pltpu.PrefetchScalarGridSpec(
            num_scalar_prefetch=1,
            grid=(part // tile,),
            in_specs=in_specs,
            out_specs=out_specs,
            scratch_shapes=scratch,
        ),
        input_output_aliases=aliases,
        compiler_params=params_of(34),
        cost_estimate=pl.CostEstimate(
            flops=part * width * 20, bytes_accessed=moved, transcendentals=0
        ),
        name="step",
    )(me, *operands)
    sent = list(result[:2]) if slots else None
    rest = list(result[2:] if slots else result)
    return sent, rest[:3] if finishes else None, rest[3] if brings is not None else stats


def weighted_kernel(extent, factor, cols, summed, *refs):
    *totals, rows_out, stats, weighted, level = refs
    i = pl.program_id(0)

    @pl.when(i == 0)
    def _():
        weighted[...] = jnp.zeros_like(weighted)
        level[...] = jnp.zeros_like(level)

    total = tree_sum([x[...] for x in totals])
    row_new = decay_rate * factor[...] + (1.0 - decay_rate) * (total / extent + tiny_eps)
    rows_out[...] = row_new
    level[...] += row_new
    inverse = jnp.transpose(1.0 / row_new)[:, 0:1]
    part = summed.shape[1]
    for half in range(2):
        for r in range(0, part, sublanes):
            x = summed[half, r : r + sublanes]
            at = half * part + r
            weighted[...] += x * x * inverse[at : at + sublanes]

    @pl.when(i == pl.num_programs(0) - 1)
    def _():
        stats[...] = jnp.zeros_like(stats)
        stats[0:1] = jnp.sum(cols[...], axis=0, keepdims=True)
        stats[1:2] = jnp.sum(weighted[...], axis=0, keepdims=True)
        total = jnp.sum(level[0:1], axis=1, keepdims=True)
        stats[2:3] = jnp.broadcast_to(total, (1, stats.shape[1]))


def weighted_sums(extent, totals, factor, cols, summed):
    count, _, part, width = summed.shape
    along = pl.BlockSpec((None, sublanes, 2 * part), lambda i: (i, 0, 0))
    whole = pl.BlockSpec((sublanes, width), lambda i: (0, 0))
    return pl.pallas_call(
        functools.partial(weighted_kernel, extent),
        grid=(count,),
        in_specs=[
            pl.BlockSpec((None, 1, 2 * part), lambda i: (i, 0, 0)),
            whole,
            pl.BlockSpec((None, 2, part, width), lambda i: (i, 0, 0, 0)),
        ]
        + [along] * len(totals),
        out_specs=[along, whole],
        out_shape=[
            jax.ShapeDtypeStruct(totals[0].shape, f32),
            jax.ShapeDtypeStruct((sublanes, width), f32),
        ],
        scratch_shapes=[pltpu.VMEM((sublanes, width), f32), pltpu.VMEM((sublanes, 2 * part), f32)],
        compiler_params=params_of(16),
        cost_estimate=pl.CostEstimate(
            flops=3 * summed.size, bytes_accessed=4 * summed.size, transcendentals=0
        ),
        name="weighted",
    )(factor.reshape(count, 1, 2 * part), cols, summed, *totals)


def column_kernel(extent, factor, *refs):
    *parts, cols_out, pair = refs
    stats = tree_sum([x[...] for x in parts])
    col_new = decay_rate * factor[...] + (1.0 - decay_rate) * (stats[0:1] / extent + tiny_eps)
    cols_out[...] = col_new
    total = jnp.sum(stats[1:2] / col_new, axis=1, keepdims=True)
    pair[...] = jnp.zeros_like(pair)
    pair[0:1] = jnp.broadcast_to(total, (1, lanes))
    pair[1:2] = stats[2:3, :lanes] / extent


def column_stage(extent, factor, parts):
    return pl.pallas_call(
        functools.partial(column_kernel, extent),
        in_specs=[pl.BlockSpec(memory_space=pltpu.VMEM)] * (1 + len(parts)),
        out_specs=[pl.BlockSpec(memory_space=pltpu.VMEM)] * 2,
        out_shape=[
            jax.ShapeDtypeStruct(factor.shape, f32),
            jax.ShapeDtypeStruct((sublanes, lanes), f32),
        ],
        compiler_params=params_of(4),
        name="column",
    )(factor, *parts)


def finish_kernel(m, extent, row_new, col_new, total, pair, summed, params, *refs):
    new_params, update, column, by_col = refs[-4:]
    count, _, part, width = summed.shape
    row_level = pair[1:2, 0:1]
    spread = jnp.sqrt(total[0:1, 0:1] * row_level / (extent * extent))
    factor = jnp.sqrt(row_level) / jnp.maximum(1.0, spread / clip_limit)
    by_col[...] = lax.rsqrt(col_new[...])
    for i in range(count):
        column[i] = jnp.transpose(lax.rsqrt(row_new[i]) * factor)

    def body(p, new_p, moved):
        i = pl.program_id(0)
        for half in range(2):
            for r in range(0, part, sublanes):
                at = half * part + r
                mine = column[i, at : at + sublanes][:, 0:1]
                y = summed[i, half, r : r + sublanes] * mine * by_col[...]
                moved[half, r : r + sublanes] = y
                new_p[half, r : r + sublanes] = p[half, r : r + sublanes] - learn_rate * y

    of_matrix = pl.BlockSpec((None, None, 2, part, width), lambda i: (m, i, 0, 0, 0))
    pltpu.emit_pipeline(
        body, grid=(count,), in_specs=[of_matrix], out_specs=[of_matrix] * 2
    )(params, new_params, update)


def finish(m, extent, row_new, col_new, pair, summed, params, outs, mib):
    count, _, part, width = summed.shape
    held = () if outs is None else outs
    in_hbm = pl.BlockSpec(memory_space=pltpu.HBM)
    in_vmem = pl.BlockSpec(memory_space=pltpu.VMEM)
    return pl.pallas_call(
        functools.partial(finish_kernel, m, extent),
        in_specs=[in_vmem] * 5 + [in_hbm] * (1 + len(held)),
        out_specs=[in_hbm] * 2,
        out_shape=[jax.ShapeDtypeStruct(params.shape, f32)] * 2,
        scratch_shapes=[
            pltpu.VMEM((count, 2 * part, sublanes), f32),
            pltpu.VMEM((1, width), f32),
        ],
        input_output_aliases={6 + i: i for i in range(len(held))},
        compiler_params=params_of(mib),
        cost_estimate=pl.CostEstimate(
            flops=4 * summed.size, bytes_accessed=16 * summed.size, transcendentals=0
        ),
        name="finish",
    )(row_new, col_new, *pair, summed, params, *held)


def per_device(partials, params, row_factor, col_factor):
    mats, rows, block_cols = params.shape
    extent = block_cols * lax.axis_size("col")
    me = lax.axis_index("dp").astype(jnp.int32).reshape(1)
    count = blocks_of_matrix
    part = rows // (2 * count)
    total_blocks = mats * count
    pieces = partials.reshape(mats, partials.shape[2], count, 2, part, block_cols)
    blocked = params.reshape(mats, count, 2, part, block_cols)
    new_rows, new_columns = [], []

    def row_stage(m, sums):
        cols, summed, rows_along = sums
        row_new, stats = weighted_sums(
            extent, [pairwise_sum(rows_along, "col")], row_factor[m], cols, summed
        )
        new_rows.append(row_new[:, 0].reshape(rows))
        return row_new, pairwise_sum(stats, "row")

    def col_stage(m, parts):
        col_new, pair = column_stage(extent, col_factor[m : m + 1], parts)
        new_columns.append(col_new)
        total = pairwise_sum(pair[0:1], "col")
        return col_new, (total, pair)

    flying = {}
    sums = stats = outs = None
    last = {}
    for j in range(-2, total_blocks + 2):
        m, b = divmod(j - 2, count)
        since = b + 1 if m >= 1 else None
        carries = {1: 0, 3: 1}.get(since)
        brings = {3: 0, 5: 1}.get(since)
        got = flying.pop(j, None)
        sent, sums, stats = step(
            j, total_blocks, me, pieces, got, sums, stats, brings, carries
        )
        if sent is not None:
            flying[j + 2] = [swap(sent[0], "dp", 1), swap(sent[1], "dp", 2)]
        if sums:
            me, *sums = tie(me, *sums)
        else:
            me, *_ = tie(me, *sent)
        if 0 <= m < mats - 1 and b == count - 1:
            row_new, stats = row_stage(m, sums)
            last = dict(m=m, row_new=row_new, summed=sums[1])
            me, stats = tie(me, stats)
        if since == 5:
            stats, me = tie(stats, me)
            col_new, pairs = col_stage(last["m"], [stats])
            outs = finish(
                last["m"], extent, last["row_new"], col_new, pairs, last["summed"], blocked, outs, 36
            )
            me, *outs = tie(me, *outs)

    row_new, stats = row_stage(mats - 1, sums)
    col_new, pairs = col_stage(mats - 1, exchange(stats, "dp"))
    new_params, update = finish(
        mats - 1, extent, row_new, col_new, pairs, sums[1], blocked, outs, 44
    )
    return (
        new_params.reshape(params.shape),
        update.reshape(params.shape),
        jnp.stack(new_rows),
        jnp.concatenate(new_columns, axis=0),
    )


def solution(mesh):
    placed = (
        P("dp", None, None, "row", None, "col"),
        P(None, ("dp", "row"), "col"),
        P(None, ("dp", "row")),
        P(None, "col"),
    )
    return jax.shard_map(
        per_device,
        mesh=mesh,
        in_specs=placed,
        out_specs=(
            P(None, ("dp", "row"), "col"),
            P(None, ("dp", "row"), "col"),
            P(None, ("dp", "row")),
            P(None, "col"),
        ),
        check_vma=False,
    )
```

```python
import functools

import jax
import jax.numpy as jnp
from jax import lax
from jax.experimental import pallas as pl
from jax.experimental.pallas import tpu as pltpu
from jax.sharding import PartitionSpec as P

decay_rate = 1.0 - 2.0 ** (-0.8)
tiny_eps = 1e-30
clip_limit = 1.0
learn_rate = 0.01

lanes = 128
sublanes = 8
blocks_of_matrix = 8
tile_rows = 16
f32 = jnp.float32


def swap(x, axes, mask):
    size = lax.axis_size(axes)
    return lax.ppermute(x, axes, [(i, i ^ mask) for i in range(size)])


def exchange(x, axes):
    return [x] + [swap(x, axes, mask) for mask in range(1, lax.axis_size(axes))]


def tree_sum(got):
    while len(got) > 1:
        got = [got[i] + got[i + 1] for i in range(0, len(got), 2)]
    return got[0]


def pairwise_sum(x, axes):
    mask = 1
    while mask < lax.axis_size(axes):
        x = x + swap(x, axes, mask)
        mask *= 2
    return x


def tie(*xs):
    return lax.optimization_barrier(xs)


def params_of(mib):
    return pltpu.CompilerParams(vmem_limit_bytes=mib * 1024 * 1024)


def step_kernel(takes, finishes, b, sends, starts, brings, carries, *refs):
    refs = list(refs[1:])
    take = lambda yes: refs.pop(0) if yes else None
    got = [take(takes or finishes) for _ in range(2)]
    mine = take(finishes)
    direct = [take(sends) for _ in range(2)]
    relay = [take(sends) for _ in range(2)]
    onward = take(starts)
    first = b == 0
    again = finishes and not first
    cols_in, rows_in, _ = take(again), take(again), take(again)
    stats_in = take(brings is not None or carries is not None)
    out = [take(sends or starts) for _ in range(2)]
    cols_out, rows_out, summed_out = take(finishes), take(finishes), take(finishes)
    stats_out = take(brings is not None)
    row_parts = take(finishes)
    t = pl.program_id(0)
    tile, width = (onward if starts else mine if finishes else direct[0]).shape[-2:]
    part = tile * pl.num_programs(0)

    def rows_of(slot):
        return pl.ds(pl.multiple_of(slot * part + t * tile, sublanes), tile)

    @pl.when(t == 0)
    def _():
        if finishes:
            cols_out[...] = jnp.zeros_like(cols_out) if first else cols_in[...]
            rows_out[...] = jnp.zeros_like(rows_out) if first else rows_in[...]
        if brings is not None:
            brought = got[brings][got[brings].shape[0] - sublanes :, : stats_in.shape[1]]
            stats_out[...] = stats_in[...] + brought
        if carries is not None:
            stats = stats_in if brings is None else stats_out
            out[carries][out[carries].shape[0] - sublanes :, : stats.shape[1]] = stats[...]

    for half in range(2):
        if starts:
            out[half][rows_of(2 if sends else 0)] = onward[half].astype(f32)
        if sends:
            out[half][rows_of(0)] = direct[half][...].astype(f32)
            passed = got[half][rows_of(2 if finishes else 0)]
            out[1 - half][rows_of(1)] = passed + relay[half][...].astype(f32)
        if finishes:
            total = mine[half].astype(f32) + got[half][rows_of(0)] + got[1 - half][rows_of(1)]
            summed_out[half] = total
            squares = total * total
            row_parts[rows_of(half)] = sum(squares[:, i : i + lanes] for i in range(0, width, lanes))
            cols_out[...] += sum(squares[i : i + sublanes] for i in range(0, tile, sublanes))

    if finishes:

        @pl.when(t == pl.num_programs(0) - 1)
        def _():
            along = lax.dot_general(
                jnp.ones((sublanes, lanes), f32),
                row_parts[...],
                (((1,), (1,)), ((), ())),
                precision=lax.Precision.HIGHEST,
                preferred_element_type=f32,
            )
            rows_out[b : b + 1] = along[0:1]


def step(j, total_blocks, me, partials, got, sums, stats, brings, carries):
    mats, _, count, _, part, width = partials.shape
    tile = min(tile_rows, part)
    finishes = j >= 2
    takes = 0 <= j < total_blocks
    sends = takes
    starts = j + 2 < total_blocks
    b = (j - 2) % count
    first = finishes and b == 0

    def piece_spec(block, mask, half):
        m, b = divmod(block, count)
        if half is None:
            return pl.BlockSpec(
                (None, None, None, 2, tile, width),
                lambda t, at: (m, at[0] ^ mask, b, 0, t, 0),
            )
        return pl.BlockSpec(
            (None, None, None, None, tile, width),
            lambda t, at: (m, at[0] ^ mask, b, half, t, 0),
        )

    in_vmem = pl.BlockSpec(memory_space=pltpu.VMEM)
    operands, in_specs = [], []

    def add(x, spec):
        operands.append(x)
        in_specs.append(spec)

    if j >= 0:
        for x in got:
            add(x, in_vmem)
    if finishes:
        add(partials, piece_spec(j - 2, 0, None))
    if sends:
        for half, mask in ((0, 1), (1, 2)):
            add(partials, piece_spec(j, mask, half))
        for half, mask in ((0, 2), (1, 1)):
            add(partials, piece_spec(j, mask, half))
    if starts:
        add(partials, piece_spec(j + 2, 3, None))

    slots = (2 if sends else 0) + (1 if starts else 0)
    out_shape, out_specs, scratch, aliases = [], [], [], {}
    if slots:
        for link in range(2):
            size = slots * part + (sublanes if link == carries else 0)
            out_shape.append(jax.ShapeDtypeStruct((size, width), f32))
            out_specs.append(in_vmem)
    whole = lambda *shape: pl.BlockSpec(shape, lambda t, at: (0,) * len(shape))
    if finishes:
        rows_shape = (count, 2 * part)
        if not first:
            add(sums[0], whole(sublanes, width))
            add(sums[1], whole(*rows_shape))
            aliases[1 + len(operands)] = len(out_shape) + 2
            add(sums[2], pl.BlockSpec(memory_space=pl.ANY))
        out_shape.append(jax.ShapeDtypeStruct((sublanes, width), f32))
        out_specs.append(whole(sublanes, width))
        out_shape.append(jax.ShapeDtypeStruct(rows_shape, f32))
        out_specs.append(whole(*rows_shape))
        out_shape.append(jax.ShapeDtypeStruct((count, 2, part, width), f32))
        out_specs.append(pl.BlockSpec((None, 2, tile, width), lambda t, at: (b, 0, t, 0)))
        scratch.append(pltpu.VMEM((2 * part, lanes), f32))
    if brings is not None or carries is not None:
        add(stats, whole(*stats.shape))
    if brings is not None:
        out_shape.append(jax.ShapeDtypeStruct(stats.shape, f32))
        out_specs.append(whole(*stats.shape))
    moved = part * width * (4 * (2 * slots + 8) + 2 * 8)
    result = pl.pallas_call(
        functools.partial(step_kernel, takes, finishes, b, sends, starts, brings, carries),
        out_shape=out_shape,
        grid_spec=pltpu.PrefetchScalarGridSpec(
            num_scalar_prefetch=1,
            grid=(part // tile,),
            in_specs=in_specs,
            out_specs=out_specs,
            scratch_shapes=scratch,
        ),
        input_output_aliases=aliases,
        compiler_params=params_of(34),
        cost_estimate=pl.CostEstimate(
            flops=part * width * 20, bytes_accessed=moved, transcendentals=0
        ),
        name="step",
    )(me, *operands)
    sent = list(result[:2]) if slots else None
    rest = list(result[2:] if slots else result)
    return sent, rest[:3] if finishes else None, rest[3] if brings is not None else stats


def weighted_kernel(extent, factor, cols, summed, *refs):
    *totals, rows_out, stats, weighted = refs
    count, _, part, width = summed.shape
    total = tree_sum([x[...] for x in totals])
    row_new = decay_rate * factor[...] + (1.0 - decay_rate) * (total / extent + tiny_eps)
    rows_out[...] = row_new
    inverse = jnp.transpose(1.0 / row_new)
    weighted[...] = jnp.zeros_like(weighted)
    for i in range(count):
        for r in range(0, 2 * part, sublanes):
            half, at = divmod(r, part)
            x = summed[i, half, at : at + sublanes]
            weighted[...] += x * x * inverse[r : r + sublanes, i : i + 1]
    size = width // sublanes
    for at, x in ((0, cols), (size, weighted)):
        sums = jnp.sum(x[...], axis=0, keepdims=True)
        for k in range(sublanes):
            stats[k : k + 1, at : at + size] = sums[:, k * size : (k + 1) * size]
    level = jnp.sum(jnp.sum(row_new, axis=0, keepdims=True), axis=1, keepdims=True)
    stats[:, 2 * size :] = jnp.broadcast_to(level, (sublanes, lanes))


def weighted_sums(extent, totals, factor, cols, summed):
    width = summed.shape[-1]
    in_vmem = pl.BlockSpec(memory_space=pltpu.VMEM)
    return pl.pallas_call(
        functools.partial(weighted_kernel, extent),
        in_specs=[in_vmem] * (3 + len(totals)),
        out_specs=[in_vmem] * 2,
        out_shape=[
            jax.ShapeDtypeStruct(totals[0].shape, f32),
            jax.ShapeDtypeStruct((sublanes, 2 * width // sublanes + lanes), f32),
        ],
        scratch_shapes=[pltpu.VMEM((sublanes, width), f32)],
        compiler_params=params_of(16),
        cost_estimate=pl.CostEstimate(
            flops=3 * summed.size, bytes_accessed=4 * summed.size, transcendentals=0
        ),
        name="weighted",
    )(factor.reshape(totals[0].shape), cols, summed, *totals)


def column_kernel(extent, factor, *refs):
    *parts, cols_out, pair = refs
    stats = tree_sum([x[...] for x in parts])
    size = factor.shape[1]
    col_new = decay_rate * factor[...] + (1.0 - decay_rate) * (stats[:, :size] / extent + tiny_eps)
    cols_out[...] = col_new
    total = jnp.sum(stats[:, size : 2 * size] / col_new, axis=0, keepdims=True)
    total = jnp.sum(total, axis=1, keepdims=True)
    pair[...] = stats[:, 2 * size :] / extent
    pair[0:1] = jnp.broadcast_to(total, (1, lanes))


def column_stage(extent, factor, parts):
    return pl.pallas_call(
        functools.partial(column_kernel, extent),
        in_specs=[pl.BlockSpec(memory_space=pltpu.VMEM)] * (1 + len(parts)),
        out_specs=[pl.BlockSpec(memory_space=pltpu.VMEM)] * 2,
        out_shape=[
            jax.ShapeDtypeStruct(factor.shape, f32),
            jax.ShapeDtypeStruct((sublanes, lanes), f32),
        ],
        compiler_params=params_of(4),
        name="column",
    )(factor, *parts)


def finish_kernel(m, extent, partners, staged, row_new, col_new, summed, params, *refs):
    pairs, (new_params, update, column, by_col) = refs[:partners], refs[-4:]
    count, _, part, width = summed.shape
    row_level = pairs[0][1:2, 0:1]
    total = tree_sum([x[0:1, 0:1] for x in pairs]) * row_level
    spread = jnp.sqrt(total / (extent * extent))
    factor = jnp.sqrt(row_level) / jnp.maximum(1.0, spread / clip_limit)
    by_row = jnp.transpose(lax.rsqrt(row_new[...]) * factor)
    for i in range(count):
        column[i] = jnp.broadcast_to(by_row[:, i : i + 1], column.shape[1:])
    size = width // sublanes
    for k in range(sublanes):
        by_col[:, k * size : (k + 1) * size] = lax.rsqrt(col_new[k : k + 1])

    def body(*blocks):
        i = pl.program_id(0)
        new_p, moved = blocks[-2:]
        for half in range(2):
            for r in range(0, part, sublanes):
                at = half * part + r
                mine = column[i, at : at + sublanes][:, 0:1]
                y = summed[i, half, r : r + sublanes] * mine * by_col[...]
                moved[half, r : r + sublanes] = y
                p = params[i, half, r : r + sublanes] if staged else blocks[0][half, r : r + sublanes]
                new_p[half, r : r + sublanes] = p - learn_rate * y

    of_matrix = pl.BlockSpec((None, None, 2, part, width), lambda i: (m, i, 0, 0, 0))
    pltpu.emit_pipeline(
        body, grid=(count,), in_specs=[] if staged else [of_matrix], out_specs=[of_matrix] * 2
    )(*([] if staged else [params]), new_params, update)


def finish(m, extent, row_new, col_new, pairs, summed, params, outs, mib):
    count, _, part, width = summed.shape
    staged = outs is not None
    held = outs if staged else ()
    in_hbm = pl.BlockSpec(memory_space=pltpu.HBM)
    in_vmem = pl.BlockSpec(memory_space=pltpu.VMEM)
    out_shape = jax.ShapeDtypeStruct(held[0].shape if staged else params.shape, f32)
    return pl.pallas_call(
        functools.partial(finish_kernel, m, extent, len(pairs), staged),
        in_specs=[in_vmem] * 3
        + [in_vmem if staged else in_hbm]
        + [in_vmem] * len(pairs)
        + [in_hbm] * len(held),
        out_specs=[in_hbm] * 2,
        out_shape=[out_shape] * 2,
        scratch_shapes=[
            pltpu.VMEM((count, 2 * part, lanes), f32),
            pltpu.VMEM((1, width), f32),
        ],
        input_output_aliases={4 + len(pairs) + i: i for i in range(len(held))},
        compiler_params=params_of(mib),
        cost_estimate=pl.CostEstimate(
            flops=4 * summed.size, bytes_accessed=16 * summed.size, transcendentals=0
        ),
        name="finish",
    )(row_new, col_new, summed, params, *pairs, *held)


def per_device(partials, params, row_factor, col_factor):
    mats, rows, block_cols = params.shape
    extent = block_cols * lax.axis_size("col")
    me = lax.axis_index("dp").astype(jnp.int32).reshape(1)
    count = blocks_of_matrix
    part = rows // (2 * count)
    total_blocks = mats * count
    pieces = partials.reshape(mats, partials.shape[2], count, 2, part, block_cols)
    blocked = params.reshape(mats, count, 2, part, block_cols)
    new_rows, new_columns = [], []

    def row_stage(m, sums):
        cols, rows_along, summed = sums
        row_new, stats = weighted_sums(
            extent, exchange(rows_along, "col"), row_factor[m], cols, summed
        )
        new_rows.append(row_new.reshape(rows))
        return row_new, pairwise_sum(stats, "row")

    def col_stage(m, parts):
        col_new, pair = column_stage(extent, col_factor[m].reshape(sublanes, -1), parts)
        new_columns.append(col_new.reshape(block_cols))
        return col_new, exchange(pair, "col")

    flying = {}
    sums = stats = outs = None
    last = {}
    for j in range(-2, total_blocks + 2):
        m, b = divmod(j - 2, count)
        since = b + 1 if m >= 1 else None
        carries = {1: 0, 3: 1}.get(since)
        brings = {3: 0, 5: 1}.get(since)
        got = flying.pop(j, None)
        sent, sums, stats = step(
            j, total_blocks, me, pieces, got, sums, stats, brings, carries
        )
        if sent is not None:
            flying[j + 2] = [swap(sent[0], "dp", 1), swap(sent[1], "dp", 2)]
        if sums:
            me, *sums = tie(me, *sums)
        else:
            me, *_ = tie(me, *sent)
        if 0 <= m < mats - 1 and b == count - 1:
            row_new, stats = row_stage(m, sums)
            last = dict(m=m, row_new=row_new, summed=sums[2])
            me, stats = tie(me, stats)
        if since == 5:
            stats, me = tie(stats, me)
            col_new, pairs = col_stage(last["m"], [stats])
            outs = finish(
                last["m"], extent, last["row_new"], col_new, pairs, last["summed"], blocked, outs, 36
            )
            me, *outs = tie(me, *outs)
        if j == total_blocks - 1:
            me, last_params = tie(me, blocked[mats - 1])

    row_new, stats = row_stage(mats - 1, sums)
    col_new, pairs = col_stage(mats - 1, exchange(stats, "dp"))
    new_params, update = finish(
        mats - 1, extent, row_new, col_new, pairs, sums[2], last_params, outs, 12
    )
    return (
        new_params.reshape(params.shape),
        update.reshape(params.shape),
        jnp.stack(new_rows),
        jnp.stack(new_columns),
    )


def solution(mesh):
    placed = (
        P("dp", None, None, "row", None, "col"),
        P(None, ("dp", "row"), "col"),
        P(None, ("dp", "row")),
        P(None, "col"),
    )
    return jax.shard_map(
        per_device,
        mesh=mesh,
        in_specs=placed,
        out_specs=(
            P(None, ("dp", "row"), "col"),
            P(None, ("dp", "row"), "col"),
            P(None, ("dp", "row")),
            P(None, "col"),
        ),
        check_vma=False,
    )
```

```python
import functools

import jax
import jax.numpy as jnp
from jax import lax
from jax.experimental import pallas as pl
from jax.experimental.pallas import tpu as pltpu
from jax.sharding import PartitionSpec as P

decay_rate = 1.0 - 2.0 ** (-0.8)
tiny_eps = 1e-30
clip_limit = 1.0
learn_rate = 0.01

lanes = 128
sublanes = 8
blocks_of_matrix = 8
tile_rows = 16
f32 = jnp.float32


def swap(x, axes, mask):
    size = lax.axis_size(axes)
    return lax.ppermute(x, axes, [(i, i ^ mask) for i in range(size)])


def exchange(x, axes):
    got = [swap(x, axes, mask) for mask in reversed(range(1, lax.axis_size(axes)))]
    return [x] + got[::-1]


def tree_sum(got):
    while len(got) > 1:
        got = [got[i] + got[i + 1] for i in range(0, len(got), 2)]
    return got[0]


def pairwise_sum(x, axes):
    mask = 1
    while mask < lax.axis_size(axes):
        x = x + swap(x, axes, mask)
        mask *= 2
    return x


def tie(*xs):
    return lax.optimization_barrier(xs)


def params_of(mib):
    return pltpu.CompilerParams(vmem_limit_bytes=mib * 1024 * 1024)


def step_kernel(takes, finishes, b, sends, starts, brings, carries, *refs):
    refs = list(refs[1:])
    take = lambda yes: refs.pop(0) if yes else None
    got = [take(takes or finishes) for _ in range(2)]
    mine = take(finishes)
    direct = [take(sends) for _ in range(2)]
    relay = [take(sends) for _ in range(2)]
    onward = take(starts)
    first = b == 0
    again = finishes and not first
    cols_in, rows_in, _ = take(again), take(again), take(again)
    stats_in = take(brings is not None or carries is not None)
    out = [take(sends or starts) for _ in range(2)]
    cols_out, rows_out, summed_out = take(finishes), take(finishes), take(finishes)
    stats_out = take(brings is not None)
    row_parts = take(finishes)
    t = pl.program_id(0)
    tile, width = (onward if starts else mine if finishes else direct[0]).shape[-2:]
    part = tile * pl.num_programs(0)

    def rows_of(slot):
        return pl.ds(pl.multiple_of(slot * part + t * tile, sublanes), tile)

    @pl.when(t == 0)
    def _():
        if finishes:
            cols_out[...] = jnp.zeros_like(cols_out) if first else cols_in[...]
            rows_out[...] = jnp.zeros_like(rows_out) if first else rows_in[...]
        if brings is not None:
            brought = got[brings][got[brings].shape[0] - sublanes :, : stats_in.shape[1]]
            stats_out[...] = stats_in[...] + brought
        if carries is not None:
            stats = stats_in if brings is None else stats_out
            out[carries][out[carries].shape[0] - sublanes :, : stats.shape[1]] = stats[...]

    for half in range(2):
        if starts:
            out[half][rows_of(2 if sends else 0)] = onward[half].astype(f32)
        if sends:
            out[half][rows_of(0)] = direct[half][...].astype(f32)
            passed = got[half][rows_of(2 if finishes else 0)]
            out[1 - half][rows_of(1)] = passed + relay[half][...].astype(f32)
        if finishes:
            total = mine[half].astype(f32) + got[half][rows_of(0)] + got[1 - half][rows_of(1)]
            summed_out[half] = total
            squares = total * total
            row_parts[rows_of(half)] = sum(squares[:, i : i + lanes] for i in range(0, width, lanes))
            cols_out[...] += sum(squares[i : i + sublanes] for i in range(0, tile, sublanes))

    if finishes:

        @pl.when(t == pl.num_programs(0) - 1)
        def _():
            along = lax.dot_general(
                jnp.ones((sublanes, lanes), f32),
                row_parts[...],
                (((1,), (1,)), ((), ())),
                precision=lax.Precision.HIGHEST,
                preferred_element_type=f32,
            )
            rows_out[b : b + 1] = along[0:1]


def step(j, total_blocks, me, partials, got, sums, stats, brings, carries):
    mats, _, count, _, part, width = partials.shape
    tile = min(tile_rows, part)
    finishes = j >= 2
    takes = 0 <= j < total_blocks
    sends = takes
    starts = j + 2 < total_blocks
    b = (j - 2) % count
    first = finishes and b == 0

    def piece_spec(block, mask, half):
        m, b = divmod(block, count)
        if half is None:
            return pl.BlockSpec(
                (None, None, None, 2, tile, width),
                lambda t, at: (m, at[0] ^ mask, b, 0, t, 0),
            )
        return pl.BlockSpec(
            (None, None, None, None, tile, width),
            lambda t, at: (m, at[0] ^ mask, b, half, t, 0),
        )

    in_vmem = pl.BlockSpec(memory_space=pltpu.VMEM)
    operands, in_specs = [], []

    def add(x, spec):
        operands.append(x)
        in_specs.append(spec)

    if j >= 0:
        for x in got:
            add(x, in_vmem)
    if finishes:
        add(partials, piece_spec(j - 2, 0, None))
    if sends:
        for half, mask in ((0, 1), (1, 2)):
            add(partials, piece_spec(j, mask, half))
        for half, mask in ((0, 2), (1, 1)):
            add(partials, piece_spec(j, mask, half))
    if starts:
        add(partials, piece_spec(j + 2, 3, None))

    slots = (2 if sends else 0) + (1 if starts else 0)
    out_shape, out_specs, scratch, aliases = [], [], [], {}
    if slots:
        for link in range(2):
            size = slots * part + (sublanes if link == carries else 0)
            out_shape.append(jax.ShapeDtypeStruct((size, width), f32))
            out_specs.append(in_vmem)
    whole = lambda *shape: pl.BlockSpec(shape, lambda t, at: (0,) * len(shape))
    if finishes:
        rows_shape = (count, 2 * part)
        if not first:
            add(sums[0], whole(sublanes, width))
            add(sums[1], whole(*rows_shape))
            aliases[1 + len(operands)] = len(out_shape) + 2
            add(sums[2], pl.BlockSpec(memory_space=pl.ANY))
        out_shape.append(jax.ShapeDtypeStruct((sublanes, width), f32))
        out_specs.append(whole(sublanes, width))
        out_shape.append(jax.ShapeDtypeStruct(rows_shape, f32))
        out_specs.append(whole(*rows_shape))
        out_shape.append(jax.ShapeDtypeStruct((count, 2, part, width), f32))
        out_specs.append(pl.BlockSpec((None, 2, tile, width), lambda t, at: (b, 0, t, 0)))
        scratch.append(pltpu.VMEM((2 * part, lanes), f32))
    if brings is not None or carries is not None:
        add(stats, whole(*stats.shape))
    if brings is not None:
        out_shape.append(jax.ShapeDtypeStruct(stats.shape, f32))
        out_specs.append(whole(*stats.shape))
    moved = part * width * (4 * (2 * slots + 8) + 2 * 8)
    result = pl.pallas_call(
        functools.partial(step_kernel, takes, finishes, b, sends, starts, brings, carries),
        out_shape=out_shape,
        grid_spec=pltpu.PrefetchScalarGridSpec(
            num_scalar_prefetch=1,
            grid=(part // tile,),
            in_specs=in_specs,
            out_specs=out_specs,
            scratch_shapes=scratch,
        ),
        input_output_aliases=aliases,
        compiler_params=params_of(20 if finishes else 34),
        cost_estimate=pl.CostEstimate(
            flops=part * width * 20, bytes_accessed=moved, transcendentals=0
        ),
        name="step",
    )(me, *operands)
    sent = list(result[:2]) if slots else None
    rest = list(result[2:] if slots else result)
    return sent, rest[:3] if finishes else None, rest[3] if brings is not None else stats


def weighted_kernel(extent, factor, cols, summed, *refs):
    *totals, rows_out, stats, weighted = refs
    count, _, part, width = summed.shape
    total = tree_sum([x[...] for x in totals])
    row_new = decay_rate * factor[...] + (1.0 - decay_rate) * (total / extent + tiny_eps)
    rows_out[...] = row_new
    inverse = jnp.transpose(1.0 / row_new)
    weighted[...] = jnp.zeros_like(weighted)
    for i in range(count):
        for r in range(0, 2 * part, sublanes):
            half, at = divmod(r, part)
            x = summed[i, half, at : at + sublanes]
            weighted[...] += x * x * inverse[r : r + sublanes, i : i + 1]
    size = width // sublanes
    for at, x in ((0, cols), (size, weighted)):
        sums = jnp.sum(x[...], axis=0, keepdims=True)
        for k in range(sublanes):
            stats[k : k + 1, at : at + size] = sums[:, k * size : (k + 1) * size]
    level = jnp.sum(jnp.sum(row_new, axis=0, keepdims=True), axis=1, keepdims=True)
    stats[:, 2 * size :] = jnp.broadcast_to(level, (sublanes, lanes))


def weighted_sums(extent, totals, factor, cols, summed):
    width = summed.shape[-1]
    in_vmem = pl.BlockSpec(memory_space=pltpu.VMEM)
    return pl.pallas_call(
        functools.partial(weighted_kernel, extent),
        in_specs=[in_vmem] * (3 + len(totals)),
        out_specs=[in_vmem] * 2,
        out_shape=[
            jax.ShapeDtypeStruct(totals[0].shape, f32),
            jax.ShapeDtypeStruct((sublanes, 2 * width // sublanes + lanes), f32),
        ],
        scratch_shapes=[pltpu.VMEM((sublanes, width), f32)],
        compiler_params=params_of(4),
        cost_estimate=pl.CostEstimate(
            flops=3 * summed.size, bytes_accessed=4 * summed.size, transcendentals=0
        ),
        name="weighted",
    )(factor.reshape(totals[0].shape), cols, summed, *totals)


def column_kernel(extent, factor, *refs):
    *parts, cols_out, pair = refs
    stats = tree_sum([x[...] for x in parts])
    size = factor.shape[1]
    col_new = decay_rate * factor[...] + (1.0 - decay_rate) * (stats[:, :size] / extent + tiny_eps)
    cols_out[...] = col_new
    total = jnp.sum(stats[:, size : 2 * size] / col_new, axis=0, keepdims=True)
    total = jnp.sum(total, axis=1, keepdims=True)
    pair[...] = stats[:, 2 * size :] / extent
    pair[0:1] = jnp.broadcast_to(total, (1, lanes))


def column_stage(extent, factor, parts):
    return pl.pallas_call(
        functools.partial(column_kernel, extent),
        in_specs=[pl.BlockSpec(memory_space=pltpu.VMEM)] * (1 + len(parts)),
        out_specs=[pl.BlockSpec(memory_space=pltpu.VMEM)] * 2,
        out_shape=[
            jax.ShapeDtypeStruct(factor.shape, f32),
            jax.ShapeDtypeStruct((sublanes, lanes), f32),
        ],
        compiler_params=params_of(4),
        name="column",
    )(factor, *parts)


def finish_kernel(m, extent, partners, staged, row_new, col_new, summed, params, *refs):
    pairs, (new_params, update, column, by_col) = refs[:partners], refs[-4:]
    count, _, part, width = summed.shape
    row_level = pairs[0][1:2, 0:1]
    total = tree_sum([x[0:1, 0:1] for x in pairs]) * row_level
    spread = jnp.sqrt(total / (extent * extent))
    factor = jnp.sqrt(row_level) / jnp.maximum(1.0, spread / clip_limit)
    by_row = jnp.transpose(lax.rsqrt(row_new[...]) * factor)
    for i in range(count):
        column[i] = jnp.broadcast_to(by_row[:, i : i + 1], column.shape[1:])
    size = width // sublanes
    for k in range(sublanes):
        by_col[:, k * size : (k + 1) * size] = lax.rsqrt(col_new[k : k + 1])

    def body(*blocks):
        i = pl.program_id(0)
        new_p, moved = blocks[-2:]
        for half in range(2):
            for r in range(0, part, sublanes):
                at = half * part + r
                mine = column[i, at : at + sublanes][:, 0:1]
                y = summed[i, half, r : r + sublanes] * mine * by_col[...]
                moved[half, r : r + sublanes] = y
                p = params[i, half, r : r + sublanes] if staged else blocks[0][half, r : r + sublanes]
                new_p[half, r : r + sublanes] = p - learn_rate * y

    of_matrix = pl.BlockSpec((None, None, 2, part, width), lambda i: (m, i, 0, 0, 0))
    pltpu.emit_pipeline(
        body, grid=(count,), in_specs=[] if staged else [of_matrix], out_specs=[of_matrix] * 2
    )(*([] if staged else [params]), new_params, update)


def finish(m, extent, row_new, col_new, pairs, summed, params, outs, mib):
    count, _, part, width = summed.shape
    staged = outs is not None
    held = outs if staged else ()
    in_hbm = pl.BlockSpec(memory_space=pltpu.HBM)
    in_vmem = pl.BlockSpec(memory_space=pltpu.VMEM)
    out_shape = jax.ShapeDtypeStruct(held[0].shape if staged else params.shape, f32)
    return pl.pallas_call(
        functools.partial(finish_kernel, m, extent, len(pairs), staged),
        in_specs=[in_vmem] * 3
        + [in_vmem if staged else in_hbm]
        + [in_vmem] * len(pairs)
        + [in_hbm] * len(held),
        out_specs=[in_hbm] * 2,
        out_shape=[out_shape] * 2,
        scratch_shapes=[
            pltpu.VMEM((count, 2 * part, lanes), f32),
            pltpu.VMEM((1, width), f32),
        ],
        input_output_aliases={4 + len(pairs) + i: i for i in range(len(held))},
        compiler_params=params_of(mib),
        cost_estimate=pl.CostEstimate(
            flops=4 * summed.size, bytes_accessed=16 * summed.size, transcendentals=0
        ),
        name="finish",
    )(row_new, col_new, summed, params, *pairs, *held)


def per_device(partials, params, row_factor, col_factor):
    mats, rows, block_cols = params.shape
    extent = block_cols * lax.axis_size("col")
    me = lax.axis_index("dp").astype(jnp.int32).reshape(1)
    count = blocks_of_matrix
    part = rows // (2 * count)
    total_blocks = mats * count
    pieces = partials.reshape(mats, partials.shape[2], count, 2, part, block_cols)
    blocked = params.reshape(mats, count, 2, part, block_cols)
    new_rows, new_columns = [], []

    def row_stage(m, sums):
        cols, rows_along, summed = sums
        row_new, stats = weighted_sums(
            extent, exchange(rows_along, "col"), row_factor[m], cols, summed
        )
        new_rows.append(row_new.reshape(rows))
        return row_new, pairwise_sum(stats, "row")

    def col_stage(m, parts):
        col_new, pair = column_stage(extent, col_factor[m].reshape(sublanes, -1), parts)
        new_columns.append(col_new.reshape(block_cols))
        return col_new, exchange(pair, "col")

    flying = {}
    sums = stats = outs = None
    last = {}
    for j in range(-2, total_blocks + 2):
        m, b = divmod(j - 2, count)
        since = b + 1 if m >= 1 else None
        carries = {1: 0, 3: 1}.get(since)
        brings = {3: 0, 5: 1}.get(since)
        got = flying.pop(j, None)
        sent, sums, stats = step(
            j, total_blocks, me, pieces, got, sums, stats, brings, carries
        )
        if sent is not None:
            flying[j + 2] = [swap(sent[0], "dp", 1), swap(sent[1], "dp", 2)]
        if sums:
            me, *sums = tie(me, *sums)
        else:
            me, *_ = tie(me, *sent)
        if 0 <= m < mats - 1 and b == count - 1:
            row_new, stats = row_stage(m, sums)
            last = dict(m=m, row_new=row_new, summed=sums[2])
            me, stats = tie(me, stats)
        if since == 5:
            stats, me = tie(stats, me)
            col_new, pairs = col_stage(last["m"], [stats])
            outs = finish(
                last["m"], extent, last["row_new"], col_new, pairs, last["summed"], blocked, outs, 24
            )
            me, *outs = tie(me, *outs)
        if j == total_blocks - 1:
            me, last_params = tie(me, blocked[mats - 1])

    row_new, stats = row_stage(mats - 1, sums)
    col_new, pairs = col_stage(mats - 1, exchange(stats, "dp"))
    new_params, update = finish(
        mats - 1, extent, row_new, col_new, pairs, sums[2], last_params, outs, 12
    )
    return (
        new_params.reshape(params.shape),
        update.reshape(params.shape),
        jnp.stack(new_rows),
        jnp.stack(new_columns),
    )


def solution(mesh):
    placed = (
        P("dp", None, None, "row", None, "col"),
        P(None, ("dp", "row"), "col"),
        P(None, ("dp", "row")),
        P(None, "col"),
    )
    return jax.shard_map(
        per_device,
        mesh=mesh,
        in_specs=placed,
        out_specs=(
            P(None, ("dp", "row"), "col"),
            P(None, ("dp", "row"), "col"),
            P(None, ("dp", "row")),
            P(None, "col"),
        ),
        check_vma=False,
    )
```

```python
import functools

import jax
import jax.numpy as jnp
from jax import lax
from jax.experimental import pallas as pl
from jax.experimental.pallas import tpu as pltpu
from jax.sharding import PartitionSpec as P

decay_rate = 1.0 - 2.0 ** (-0.8)
tiny_eps = 1e-30
clip_limit = 1.0
learn_rate = 0.01

lanes = 128
sublanes = 8
blocks_of_matrix = 8
tile_rows = 16
f32 = jnp.float32


def swap(x, axes, mask):
    size = lax.axis_size(axes)
    return lax.ppermute(x, axes, [(i, i ^ mask) for i in range(size)])


def exchange(x, axes):
    got = [swap(x, axes, mask) for mask in reversed(range(1, lax.axis_size(axes)))]
    return [x] + got[::-1]


def tree_sum(got):
    while len(got) > 1:
        got = [got[i] + got[i + 1] for i in range(0, len(got), 2)]
    return got[0]


def pairwise_sum(x, axes):
    mask = 1
    while mask < lax.axis_size(axes):
        x = x + swap(x, axes, mask)
        mask *= 2
    return x


def tie(*xs):
    return lax.optimization_barrier(xs)


def params_of(mib):
    return pltpu.CompilerParams(vmem_limit_bytes=mib * 1024 * 1024)


def step_kernel(takes, finishes, b, sends, starts, brings, carries, *refs):
    refs = list(refs[1:])
    take = lambda yes: refs.pop(0) if yes else None
    got = [take(takes or finishes) for _ in range(2)]
    mine = take(finishes)
    direct = [take(sends) for _ in range(2)]
    relay = [take(sends) for _ in range(2)]
    onward = take(starts)
    first = b == 0
    again = finishes and not first
    cols_in, rows_in, _ = take(again), take(again), take(again)
    stats_in = take(brings is not None or carries is not None)
    out = [take(sends or starts) for _ in range(2)]
    cols_out, rows_out, summed_out = take(finishes), take(finishes), take(finishes)
    stats_out = take(brings is not None)
    row_parts = take(finishes)
    t = pl.program_id(0)
    tile, width = (onward if starts else mine if finishes else direct[0]).shape[-2:]
    part = tile * pl.num_programs(0)

    def rows_of(slot):
        return pl.ds(pl.multiple_of(slot * part + t * tile, sublanes), tile)

    @pl.when(t == 0)
    def _():
        if finishes:
            cols_out[...] = jnp.zeros_like(cols_out) if first else cols_in[...]
            rows_out[...] = jnp.zeros_like(rows_out) if first else rows_in[...]
        if brings is not None:
            brought = got[brings][got[brings].shape[0] - sublanes :, : stats_in.shape[1]]
            stats_out[...] = stats_in[...] + brought
        if carries is not None:
            stats = stats_in if brings is None else stats_out
            out[carries][out[carries].shape[0] - sublanes :, : stats.shape[1]] = stats[...]

    for half in range(2):
        if starts:
            out[half][rows_of(2 if sends else 0)] = onward[half].astype(f32)
        if sends:
            out[half][rows_of(0)] = direct[half][...].astype(f32)
            passed = got[half][rows_of(2 if finishes else 0)]
            out[1 - half][rows_of(1)] = passed + relay[half][...].astype(f32)
        if finishes:
            total = mine[half].astype(f32) + got[half][rows_of(0)] + got[1 - half][rows_of(1)]
            summed_out[half] = total
            squares = total * total
            row_parts[rows_of(half)] = sum(squares[:, i : i + lanes] for i in range(0, width, lanes))
            cols_out[...] += sum(squares[i : i + sublanes] for i in range(0, tile, sublanes))

    if finishes:

        @pl.when(t == pl.num_programs(0) - 1)
        def _():
            along = lax.dot_general(
                jnp.ones((sublanes, lanes), f32),
                row_parts[...],
                (((1,), (1,)), ((), ())),
                precision=lax.Precision.HIGHEST,
                preferred_element_type=f32,
            )
            rows_out[b : b + 1] = along[0:1]


def step(j, total_blocks, me, partials, got, sums, stats, brings, carries):
    mats, _, count, _, part, width = partials.shape
    finishes = j >= 2
    takes = 0 <= j < total_blocks
    tile = min(tile_rows if takes else 2 * tile_rows, part)
    sends = takes
    starts = j + 2 < total_blocks
    b = (j - 2) % count
    first = finishes and b == 0

    def piece_spec(block, mask, half):
        m, b = divmod(block, count)
        if half is None:
            return pl.BlockSpec(
                (None, None, None, 2, tile, width),
                lambda t, at: (m, at[0] ^ mask, b, 0, t, 0),
            )
        return pl.BlockSpec(
            (None, None, None, None, tile, width),
            lambda t, at: (m, at[0] ^ mask, b, half, t, 0),
        )

    in_vmem = pl.BlockSpec(memory_space=pltpu.VMEM)
    operands, in_specs = [], []

    def add(x, spec):
        operands.append(x)
        in_specs.append(spec)

    if j >= 0:
        for x in got:
            add(x, in_vmem)
    if finishes:
        add(partials, piece_spec(j - 2, 0, None))
    if sends:
        for half, mask in ((0, 1), (1, 2)):
            add(partials, piece_spec(j, mask, half))
        for half, mask in ((0, 2), (1, 1)):
            add(partials, piece_spec(j, mask, half))
    if starts:
        add(partials, piece_spec(j + 2, 3, None))

    slots = (2 if sends else 0) + (1 if starts else 0)
    out_shape, out_specs, scratch, aliases = [], [], [], {}
    if slots:
        for link in range(2):
            size = slots * part + (sublanes if link == carries else 0)
            out_shape.append(jax.ShapeDtypeStruct((size, width), f32))
            out_specs.append(in_vmem)
    whole = lambda *shape: pl.BlockSpec(shape, lambda t, at: (0,) * len(shape))
    if finishes:
        rows_shape = (count, 2 * part)
        if not first:
            add(sums[0], whole(sublanes, width))
            add(sums[1], whole(*rows_shape))
            aliases[1 + len(operands)] = len(out_shape) + 2
            add(sums[2], pl.BlockSpec(memory_space=pl.ANY))
        out_shape.append(jax.ShapeDtypeStruct((sublanes, width), f32))
        out_specs.append(whole(sublanes, width))
        out_shape.append(jax.ShapeDtypeStruct(rows_shape, f32))
        out_specs.append(whole(*rows_shape))
        out_shape.append(jax.ShapeDtypeStruct((count, 2, part, width), f32))
        out_specs.append(pl.BlockSpec((None, 2, tile, width), lambda t, at: (b, 0, t, 0)))
        scratch.append(pltpu.VMEM((2 * part, lanes), f32))
    if brings is not None or carries is not None:
        add(stats, whole(*stats.shape))
    if brings is not None:
        out_shape.append(jax.ShapeDtypeStruct(stats.shape, f32))
        out_specs.append(whole(*stats.shape))
    moved = part * width * (4 * (2 * slots + 8) + 2 * 8)
    result = pl.pallas_call(
        functools.partial(step_kernel, takes, finishes, b, sends, starts, brings, carries),
        out_shape=out_shape,
        grid_spec=pltpu.PrefetchScalarGridSpec(
            num_scalar_prefetch=1,
            grid=(part // tile,),
            in_specs=in_specs,
            out_specs=out_specs,
            scratch_shapes=scratch,
        ),
        input_output_aliases=aliases,
        compiler_params=params_of(34),
        cost_estimate=pl.CostEstimate(
            flops=part * width * 20, bytes_accessed=moved, transcendentals=0
        ),
        name="step",
    )(me, *operands)
    sent = list(result[:2]) if slots else None
    rest = list(result[2:] if slots else result)
    return sent, rest[:3] if finishes else None, rest[3] if brings is not None else stats


def weighted_kernel(extent, factor, cols, summed, *refs):
    *totals, rows_out, stats, weighted = refs
    count, _, part, width = summed.shape
    total = tree_sum([x[...] for x in totals])
    row_new = decay_rate * factor[...] + (1.0 - decay_rate) * (total / extent + tiny_eps)
    rows_out[...] = row_new
    inverse = jnp.transpose(1.0 / row_new)
    weighted[...] = jnp.zeros_like(weighted)
    for i in range(count):
        for r in range(0, 2 * part, sublanes):
            half, at = divmod(r, part)
            x = summed[i, half, at : at + sublanes]
            weighted[...] += x * x * inverse[r : r + sublanes, i : i + 1]
    size = width // sublanes
    for at, x in ((0, cols), (size, weighted)):
        sums = jnp.sum(x[...], axis=0, keepdims=True)
        for k in range(sublanes):
            stats[k : k + 1, at : at + size] = sums[:, k * size : (k + 1) * size]
    level = jnp.sum(jnp.sum(row_new, axis=0, keepdims=True), axis=1, keepdims=True)
    stats[:, 2 * size :] = jnp.broadcast_to(level, (sublanes, lanes))


def weighted_sums(extent, totals, factor, cols, summed):
    width = summed.shape[-1]
    in_vmem = pl.BlockSpec(memory_space=pltpu.VMEM)
    return pl.pallas_call(
        functools.partial(weighted_kernel, extent),
        in_specs=[in_vmem] * (3 + len(totals)),
        out_specs=[in_vmem] * 2,
        out_shape=[
            jax.ShapeDtypeStruct(totals[0].shape, f32),
            jax.ShapeDtypeStruct((sublanes, 2 * width // sublanes + lanes), f32),
        ],
        scratch_shapes=[pltpu.VMEM((sublanes, width), f32)],
        compiler_params=params_of(16),
        cost_estimate=pl.CostEstimate(
            flops=3 * summed.size, bytes_accessed=4 * summed.size, transcendentals=0
        ),
        name="weighted",
    )(factor.reshape(totals[0].shape), cols, summed, *totals)


def column_kernel(extent, factor, *refs):
    *parts, cols_out, pair = refs
    stats = tree_sum([x[...] for x in parts])
    size = factor.shape[1]
    col_new = decay_rate * factor[...] + (1.0 - decay_rate) * (stats[:, :size] / extent + tiny_eps)
    cols_out[...] = col_new
    total = jnp.sum(stats[:, size : 2 * size] / col_new, axis=0, keepdims=True)
    total = jnp.sum(total, axis=1, keepdims=True)
    pair[...] = stats[:, 2 * size :] / extent
    pair[0:1] = jnp.broadcast_to(total, (1, lanes))


def column_stage(extent, factor, parts):
    return pl.pallas_call(
        functools.partial(column_kernel, extent),
        in_specs=[pl.BlockSpec(memory_space=pltpu.VMEM)] * (1 + len(parts)),
        out_specs=[pl.BlockSpec(memory_space=pltpu.VMEM)] * 2,
        out_shape=[
            jax.ShapeDtypeStruct(factor.shape, f32),
            jax.ShapeDtypeStruct((sublanes, lanes), f32),
        ],
        compiler_params=params_of(4),
        name="column",
    )(factor, *parts)


def finish_kernel(m, extent, partners, row_new, col_new, summed, params, *refs):
    pairs, (new_params, update, column, by_col) = refs[:partners], refs[-4:]
    count, _, part, width = summed.shape

    def scale():
        row_level = pairs[0][1:2, 0:1]
        total = tree_sum([x[0:1, 0:1] for x in pairs]) * row_level
        spread = jnp.sqrt(total / (extent * extent))
        factor = jnp.sqrt(row_level) / jnp.maximum(1.0, spread / clip_limit)
        by_row = jnp.transpose(lax.rsqrt(row_new[...]) * factor)
        for i in range(count):
            column[i] = jnp.broadcast_to(by_row[:, i : i + 1], column.shape[1:])
        size = width // sublanes
        for k in range(sublanes):
            by_col[:, k * size : (k + 1) * size] = lax.rsqrt(col_new[k : k + 1])

    def body(p, new_p, moved):
        i = pl.program_id(0)
        pl.when(i == 0)(scale)
        for half in range(2):
            for r in range(0, part, sublanes):
                at = half * part + r
                mine = column[i, at : at + sublanes][:, 0:1]
                y = summed[i, half, r : r + sublanes] * mine * by_col[...]
                moved[half, r : r + sublanes] = y
                new_p[half, r : r + sublanes] = p[half, r : r + sublanes] - learn_rate * y

    of_matrix = pl.BlockSpec((None, None, 2, part, width), lambda i: (m, i, 0, 0, 0))
    pltpu.emit_pipeline(
        body, grid=(count,), in_specs=[of_matrix], out_specs=[of_matrix] * 2
    )(params, new_params, update)


def finish(m, extent, row_new, col_new, pairs, summed, params, outs, mib):
    count, _, part, width = summed.shape
    held = () if outs is None else outs
    in_hbm = pl.BlockSpec(memory_space=pltpu.HBM)
    in_vmem = pl.BlockSpec(memory_space=pltpu.VMEM)
    return pl.pallas_call(
        functools.partial(finish_kernel, m, extent, len(pairs)),
        in_specs=[in_vmem] * 3 + [in_hbm] + [in_vmem] * len(pairs) + [in_hbm] * len(held),
        out_specs=[in_hbm] * 2,
        out_shape=[jax.ShapeDtypeStruct(params.shape, f32)] * 2,
        scratch_shapes=[
            pltpu.VMEM((count, 2 * part, lanes), f32),
            pltpu.VMEM((1, width), f32),
        ],
        input_output_aliases={4 + len(pairs) + i: i for i in range(len(held))},
        compiler_params=params_of(mib),
        cost_estimate=pl.CostEstimate(
            flops=4 * summed.size, bytes_accessed=16 * summed.size, transcendentals=0
        ),
        name="finish",
    )(row_new, col_new, summed, params, *pairs, *held)


def per_device(partials, params, row_factor, col_factor):
    mats, rows, block_cols = params.shape
    extent = block_cols * lax.axis_size("col")
    me = lax.axis_index("dp").astype(jnp.int32).reshape(1)
    count = blocks_of_matrix
    part = rows // (2 * count)
    total_blocks = mats * count
    pieces = partials.reshape(mats, partials.shape[2], count, 2, part, block_cols)
    blocked = params.reshape(mats, count, 2, part, block_cols)
    new_rows, new_columns = [], []

    def row_stage(m, sums):
        cols, rows_along, summed = sums
        row_new, stats = weighted_sums(
            extent, exchange(rows_along, "col"), row_factor[m], cols, summed
        )
        new_rows.append(row_new.reshape(rows))
        return row_new, pairwise_sum(stats, "row")

    def col_stage(m, parts):
        col_new, pair = column_stage(extent, col_factor[m].reshape(sublanes, -1), parts)
        new_columns.append(col_new.reshape(block_cols))
        return col_new, exchange(pair, "col")

    flying = {}
    sums = stats = outs = None
    last = {}
    for j in range(-2, total_blocks + 2):
        m, b = divmod(j - 2, count)
        since = b + 1 if m >= 1 else None
        carries = {1: 0, 3: 1}.get(since)
        brings = {3: 0, 5: 1}.get(since)
        got = flying.pop(j, None)
        sent, sums, stats = step(
            j, total_blocks, me, pieces, got, sums, stats, brings, carries
        )
        if sent is not None:
            flying[j + 2] = [swap(sent[0], "dp", 1), swap(sent[1], "dp", 2)]
        if sums:
            me, *sums = tie(me, *sums)
        else:
            me, *_ = tie(me, *sent)
        if 0 <= m < mats - 1 and b == count - 1:
            row_new, stats = row_stage(m, sums)
            last = dict(m=m, row_new=row_new, summed=sums[2])
            me, stats = tie(me, stats)
        if since == 5:
            stats, me = tie(stats, me)
            col_new, pairs = col_stage(last["m"], [stats])
            outs = finish(
                last["m"], extent, last["row_new"], col_new, pairs, last["summed"], blocked, outs, 36
            )
            me, *outs = tie(me, *outs)

    row_new, stats = row_stage(mats - 1, sums)
    col_new, pairs = col_stage(mats - 1, exchange(stats, "dp"))
    new_params, update = finish(
        mats - 1, extent, row_new, col_new, pairs, sums[2], blocked, outs, 44
    )
    return (
        new_params.reshape(params.shape),
        update.reshape(params.shape),
        jnp.stack(new_rows),
        jnp.stack(new_columns),
    )


def solution(mesh):
    placed = (
        P("dp", None, None, "row", None, "col"),
        P(None, ("dp", "row"), "col"),
        P(None, ("dp", "row")),
        P(None, "col"),
    )
    return jax.shard_map(
        per_device,
        mesh=mesh,
        in_specs=placed,
        out_specs=(
            P(None, ("dp", "row"), "col"),
            P(None, ("dp", "row"), "col"),
            P(None, ("dp", "row")),
            P(None, "col"),
        ),
        check_vma=False,
    )
```

```python
import functools

import jax
import jax.numpy as jnp
from jax import lax
from jax.experimental import pallas as pl
from jax.experimental.pallas import tpu as pltpu
from jax.sharding import PartitionSpec as P

decay_rate = 1.0 - 2.0 ** (-0.8)
tiny_eps = 1e-30
clip_limit = 1.0
learn_rate = 0.01

lanes = 128
sublanes = 8
blocks_of_matrix = 8
tile_rows = 16
f32 = jnp.float32


def swap(x, axes, mask):
    size = lax.axis_size(axes)
    return lax.ppermute(x, axes, [(i, i ^ mask) for i in range(size)])


def exchange(x, axes):
    got = [swap(x, axes, mask) for mask in reversed(range(1, lax.axis_size(axes)))]
    return [x] + got[::-1]


def tree_sum(got):
    while len(got) > 1:
        got = [got[i] + got[i + 1] for i in range(0, len(got), 2)]
    return got[0]


def pairwise_sum(x, axes):
    mask = 1
    while mask < lax.axis_size(axes):
        x = x + swap(x, axes, mask)
        mask *= 2
    return x


def tie(*xs):
    return lax.optimization_barrier(xs)


def params_of(mib):
    return pltpu.CompilerParams(vmem_limit_bytes=mib * 1024 * 1024)


def step_kernel(takes, finishes, b, sends, starts, brings, carries, *refs):
    refs = list(refs[1:])
    take = lambda yes: refs.pop(0) if yes else None
    got = [take(takes or finishes) for _ in range(2)]
    mine = take(finishes)
    direct = [take(sends) for _ in range(2)]
    relay = [take(sends) for _ in range(2)]
    onward = take(starts)
    first = b == 0
    again = finishes and not first
    cols_in, rows_in, _ = take(again), take(again), take(again)
    stats_in = take(brings is not None or carries is not None)
    out = [take(sends or starts) for _ in range(2)]
    cols_out, rows_out, summed_out = take(finishes), take(finishes), take(finishes)
    stats_out = take(brings is not None)
    row_parts = take(finishes)
    t = pl.program_id(0)
    tile, width = (onward if starts else mine if finishes else direct[0]).shape[-2:]
    part = tile * pl.num_programs(0)

    def rows_of(slot):
        return pl.ds(pl.multiple_of(slot * part + t * tile, sublanes), tile)

    @pl.when(t == 0)
    def _():
        if finishes:
            cols_out[...] = jnp.zeros_like(cols_out) if first else cols_in[...]
            rows_out[...] = jnp.zeros_like(rows_out) if first else rows_in[...]
        if brings is not None:
            brought = got[brings][got[brings].shape[0] - sublanes :, : stats_in.shape[1]]
            stats_out[...] = stats_in[...] + brought
        if carries is not None:
            stats = stats_in if brings is None else stats_out
            out[carries][out[carries].shape[0] - sublanes :, : stats.shape[1]] = stats[...]

    for half in range(2):
        if starts:
            out[half][rows_of(2 if sends else 0)] = onward[half].astype(f32)
        if sends:
            out[half][rows_of(0)] = direct[half][...].astype(f32)
            passed = got[half][rows_of(2 if finishes else 0)]
            out[1 - half][rows_of(1)] = passed + relay[half][...].astype(f32)
        if finishes:
            total = mine[half].astype(f32) + got[half][rows_of(0)] + got[1 - half][rows_of(1)]
            summed_out[half] = total
            squares = total * total
            row_parts[rows_of(half)] = sum(squares[:, i : i + lanes] for i in range(0, width, lanes))
            cols_out[...] += sum(squares[i : i + sublanes] for i in range(0, tile, sublanes))

    if finishes:

        @pl.when(t == pl.num_programs(0) - 1)
        def _():
            along = lax.dot_general(
                jnp.ones((sublanes, lanes), f32),
                row_parts[...],
                (((1,), (1,)), ((), ())),
                precision=lax.Precision.HIGHEST,
                preferred_element_type=f32,
            )
            rows_out[b : b + 1] = along[0:1]


def step(j, total_blocks, me, partials, got, sums, stats, brings, carries):
    mats, _, count, _, part, width = partials.shape
    finishes = j >= 2
    takes = 0 <= j < total_blocks
    tile = min(tile_rows if takes else 2 * tile_rows, part)
    sends = takes
    starts = j + 2 < total_blocks
    b = (j - 2) % count
    first = finishes and b == 0

    def piece_spec(block, mask, half):
        m, b = divmod(block, count)
        if half is None:
            return pl.BlockSpec(
                (None, None, None, 2, tile, width),
                lambda t, at: (m, at[0] ^ mask, b, 0, t, 0),
            )
        return pl.BlockSpec(
            (None, None, None, None, tile, width),
            lambda t, at: (m, at[0] ^ mask, b, half, t, 0),
        )

    in_vmem = pl.BlockSpec(memory_space=pltpu.VMEM)
    operands, in_specs = [], []

    def add(x, spec):
        operands.append(x)
        in_specs.append(spec)

    if j >= 0:
        for x in got:
            add(x, in_vmem)
    if finishes:
        add(partials, piece_spec(j - 2, 0, None))
    if sends:
        for half, mask in ((0, 1), (1, 2)):
            add(partials, piece_spec(j, mask, half))
        for half, mask in ((0, 2), (1, 1)):
            add(partials, piece_spec(j, mask, half))
    if starts:
        add(partials, piece_spec(j + 2, 3, None))

    slots = (2 if sends else 0) + (1 if starts else 0)
    out_shape, out_specs, scratch, aliases = [], [], [], {}
    if slots:
        for link in range(2):
            size = slots * part + (sublanes if link == carries else 0)
            out_shape.append(jax.ShapeDtypeStruct((size, width), f32))
            out_specs.append(in_vmem)
    whole = lambda *shape: pl.BlockSpec(shape, lambda t, at: (0,) * len(shape))
    if finishes:
        rows_shape = (count, 2 * part)
        if not first:
            add(sums[0], whole(sublanes, width))
            add(sums[1], whole(*rows_shape))
            aliases[1 + len(operands)] = len(out_shape) + 2
            add(sums[2], pl.BlockSpec(memory_space=pl.ANY))
        out_shape.append(jax.ShapeDtypeStruct((sublanes, width), f32))
        out_specs.append(whole(sublanes, width))
        out_shape.append(jax.ShapeDtypeStruct(rows_shape, f32))
        out_specs.append(whole(*rows_shape))
        out_shape.append(jax.ShapeDtypeStruct((count, 2, part, width), f32))
        out_specs.append(pl.BlockSpec((None, 2, tile, width), lambda t, at: (b, 0, t, 0)))
        scratch.append(pltpu.VMEM((2 * part, lanes), f32))
    if brings is not None or carries is not None:
        add(stats, whole(*stats.shape))
    if brings is not None:
        out_shape.append(jax.ShapeDtypeStruct(stats.shape, f32))
        out_specs.append(whole(*stats.shape))
    moved = part * width * (4 * (2 * slots + 8) + 2 * 8)
    result = pl.pallas_call(
        functools.partial(step_kernel, takes, finishes, b, sends, starts, brings, carries),
        out_shape=out_shape,
        grid_spec=pltpu.PrefetchScalarGridSpec(
            num_scalar_prefetch=1,
            grid=(part // tile,),
            in_specs=in_specs,
            out_specs=out_specs,
            scratch_shapes=scratch,
        ),
        input_output_aliases=aliases,
        compiler_params=params_of(34),
        cost_estimate=pl.CostEstimate(
            flops=part * width * 20, bytes_accessed=moved, transcendentals=0
        ),
        name="step",
    )(me, *operands)
    sent = list(result[:2]) if slots else None
    rest = list(result[2:] if slots else result)
    return sent, rest[:3] if finishes else None, rest[3] if brings is not None else stats


def weighted_kernel(extent, factor, cols, summed, *refs):
    *totals, rows_out, stats, weighted, column = refs
    _, part, width = summed.shape
    i = pl.program_id(0)

    @pl.when(i == 0)
    def _():
        total = tree_sum([x[...] for x in totals])
        row_new = decay_rate * factor[...] + (1.0 - decay_rate) * (total / extent + tiny_eps)
        rows_out[...] = row_new
        inverse = jnp.transpose(1.0 / row_new)
        for k in range(column.shape[0]):
            column[k] = jnp.broadcast_to(inverse[:, k : k + 1], column.shape[1:])
        weighted[...] = jnp.zeros_like(weighted)

    for r in range(0, 2 * part, sublanes):
        half, at = divmod(r, part)
        x = summed[half, at : at + sublanes]
        weighted[...] += x * x * column[i, r : r + sublanes][:, 0:1]

    @pl.when(i == pl.num_programs(0) - 1)
    def _():
        size = width // sublanes
        for at, x in ((0, cols), (size, weighted)):
            sums = jnp.sum(x[...], axis=0, keepdims=True)
            for k in range(sublanes):
                stats[k : k + 1, at : at + size] = sums[:, k * size : (k + 1) * size]
        level = jnp.sum(jnp.sum(rows_out[...], axis=0, keepdims=True), axis=1, keepdims=True)
        stats[:, 2 * size :] = jnp.broadcast_to(level, (sublanes, lanes))


def weighted_sums(extent, totals, factor, cols, summed):
    count, _, part, width = summed.shape
    whole = lambda *shape: pl.BlockSpec(shape, lambda i: (0,) * len(shape))
    rows_shape = totals[0].shape
    stats_shape = (sublanes, 2 * width // sublanes + lanes)
    return pl.pallas_call(
        functools.partial(weighted_kernel, extent),
        grid=(count,),
        in_specs=[
            whole(*rows_shape),
            whole(*cols.shape),
            pl.BlockSpec((None, 2, part, width), lambda i: (i, 0, 0, 0)),
        ]
        + [whole(*rows_shape)] * len(totals),
        out_specs=[whole(*rows_shape), whole(*stats_shape)],
        out_shape=[
            jax.ShapeDtypeStruct(rows_shape, f32),
            jax.ShapeDtypeStruct(stats_shape, f32),
        ],
        scratch_shapes=[
            pltpu.VMEM((sublanes, width), f32),
            pltpu.VMEM((count, 2 * part, lanes), f32),
        ],
        compiler_params=params_of(16),
        cost_estimate=pl.CostEstimate(
            flops=3 * summed.size, bytes_accessed=4 * summed.size, transcendentals=0
        ),
        name="weighted",
    )(factor.reshape(rows_shape), cols, summed, *totals)


def column_kernel(extent, factor, *refs):
    *parts, cols_out, pair = refs
    stats = tree_sum([x[...] for x in parts])
    size = factor.shape[1]
    col_new = decay_rate * factor[...] + (1.0 - decay_rate) * (stats[:, :size] / extent + tiny_eps)
    cols_out[...] = col_new
    total = jnp.sum(stats[:, size : 2 * size] / col_new, axis=0, keepdims=True)
    total = jnp.sum(total, axis=1, keepdims=True)
    pair[...] = stats[:, 2 * size :] / extent
    pair[0:1] = jnp.broadcast_to(total, (1, lanes))


def column_stage(extent, factor, parts):
    return pl.pallas_call(
        functools.partial(column_kernel, extent),
        in_specs=[pl.BlockSpec(memory_space=pltpu.VMEM)] * (1 + len(parts)),
        out_specs=[pl.BlockSpec(memory_space=pltpu.VMEM)] * 2,
        out_shape=[
            jax.ShapeDtypeStruct(factor.shape, f32),
            jax.ShapeDtypeStruct((sublanes, lanes), f32),
        ],
        compiler_params=params_of(4),
        name="column",
    )(factor, *parts)


def finish_kernel(m, extent, partners, row_new, col_new, summed, params, *refs):
    pairs, (new_params, update, column, by_col) = refs[:partners], refs[-4:]
    count, _, part, width = summed.shape

    def scale():
        row_level = pairs[0][1:2, 0:1]
        total = tree_sum([x[0:1, 0:1] for x in pairs]) * row_level
        spread = jnp.sqrt(total / (extent * extent))
        factor = jnp.sqrt(row_level) / jnp.maximum(1.0, spread / clip_limit)
        by_row = jnp.transpose(lax.rsqrt(row_new[...]) * factor)
        for i in range(count):
            column[i] = jnp.broadcast_to(by_row[:, i : i + 1], column.shape[1:])
        size = width // sublanes
        for k in range(sublanes):
            by_col[:, k * size : (k + 1) * size] = lax.rsqrt(col_new[k : k + 1])

    def body(p, new_p, moved):
        i = pl.program_id(0)
        pl.when(i == 0)(scale)
        for half in range(2):
            for r in range(0, part, sublanes):
                at = half * part + r
                mine = column[i, at : at + sublanes][:, 0:1]
                y = summed[i, half, r : r + sublanes] * mine * by_col[...]
                moved[half, r : r + sublanes] = y
                new_p[half, r : r + sublanes] = p[half, r : r + sublanes] - learn_rate * y

    of_matrix = pl.BlockSpec((None, None, 2, part, width), lambda i: (m, i, 0, 0, 0))
    pltpu.emit_pipeline(
        body, grid=(count,), in_specs=[of_matrix], out_specs=[of_matrix] * 2
    )(params, new_params, update)


def finish(m, extent, row_new, col_new, pairs, summed, params, outs, mib):
    count, _, part, width = summed.shape
    held = () if outs is None else outs
    in_hbm = pl.BlockSpec(memory_space=pltpu.HBM)
    in_vmem = pl.BlockSpec(memory_space=pltpu.VMEM)
    return pl.pallas_call(
        functools.partial(finish_kernel, m, extent, len(pairs)),
        in_specs=[in_vmem] * 3 + [in_hbm] + [in_vmem] * len(pairs) + [in_hbm] * len(held),
        out_specs=[in_hbm] * 2,
        out_shape=[jax.ShapeDtypeStruct(params.shape, f32)] * 2,
        scratch_shapes=[
            pltpu.VMEM((count, 2 * part, lanes), f32),
            pltpu.VMEM((1, width), f32),
        ],
        input_output_aliases={4 + len(pairs) + i: i for i in range(len(held))},
        compiler_params=params_of(mib),
        cost_estimate=pl.CostEstimate(
            flops=4 * summed.size, bytes_accessed=16 * summed.size, transcendentals=0
        ),
        name="finish",
    )(row_new, col_new, summed, params, *pairs, *held)


def per_device(partials, params, row_factor, col_factor):
    mats, rows, block_cols = params.shape
    extent = block_cols * lax.axis_size("col")
    me = lax.axis_index("dp").astype(jnp.int32).reshape(1)
    count = blocks_of_matrix
    part = rows // (2 * count)
    total_blocks = mats * count
    pieces = partials.reshape(mats, partials.shape[2], count, 2, part, block_cols)
    blocked = params.reshape(mats, count, 2, part, block_cols)
    new_rows, new_columns = [], []

    def row_stage(m, sums):
        cols, rows_along, summed = sums
        row_new, stats = weighted_sums(
            extent, exchange(rows_along, "col"), row_factor[m], cols, summed
        )
        new_rows.append(row_new.reshape(rows))
        return row_new, pairwise_sum(stats, "row")

    def col_stage(m, parts):
        col_new, pair = column_stage(extent, col_factor[m].reshape(sublanes, -1), parts)
        new_columns.append(col_new.reshape(block_cols))
        return col_new, exchange(pair, "col")

    flying = {}
    sums = stats = outs = None
    last = {}
    for j in range(-2, total_blocks + 2):
        m, b = divmod(j - 2, count)
        since = b + 1 if m >= 1 else None
        carries = {1: 0, 3: 1}.get(since)
        brings = {3: 0, 5: 1}.get(since)
        got = flying.pop(j, None)
        sent, sums, stats = step(
            j, total_blocks, me, pieces, got, sums, stats, brings, carries
        )
        if sent is not None:
            flying[j + 2] = [swap(sent[0], "dp", 1), swap(sent[1], "dp", 2)]
        if sums:
            me, *sums = tie(me, *sums)
        else:
            me, *_ = tie(me, *sent)
        if 0 <= m < mats - 1 and b == count - 1:
            row_new, stats = row_stage(m, sums)
            last = dict(m=m, row_new=row_new, summed=sums[2])
            me, stats = tie(me, stats)
        if since == 5:
            stats, me = tie(stats, me)
            col_new, pairs = col_stage(last["m"], [stats])
            outs = finish(
                last["m"], extent, last["row_new"], col_new, pairs, last["summed"], blocked, outs, 36
            )
            me, *outs = tie(me, *outs)

    row_new, stats = row_stage(mats - 1, sums)
    col_new, pairs = col_stage(mats - 1, exchange(stats, "dp"))
    new_params, update = finish(
        mats - 1, extent, row_new, col_new, pairs, sums[2], blocked, outs, 44
    )
    return (
        new_params.reshape(params.shape),
        update.reshape(params.shape),
        jnp.stack(new_rows),
        jnp.stack(new_columns),
    )


def solution(mesh):
    placed = (
        P("dp", None, None, "row", None, "col"),
        P(None, ("dp", "row"), "col"),
        P(None, ("dp", "row")),
        P(None, "col"),
    )
    return jax.shard_map(
        per_device,
        mesh=mesh,
        in_specs=placed,
        out_specs=(
            P(None, ("dp", "row"), "col"),
            P(None, ("dp", "row"), "col"),
            P(None, ("dp", "row")),
            P(None, "col"),
        ),
        check_vma=False,
    )
```

```python
import functools

import jax
import jax.numpy as jnp
from jax import lax
from jax.experimental import pallas as pl
from jax.experimental.pallas import tpu as pltpu
from jax.sharding import PartitionSpec as P

decay_rate = 1.0 - 2.0 ** (-0.8)
tiny_eps = 1e-30
clip_limit = 1.0
learn_rate = 0.01

lanes = 128
sublanes = 8
blocks_of_matrix = 8
tile_rows = 16
f32 = jnp.float32


def swap(x, axes, mask):
    size = lax.axis_size(axes)
    return lax.ppermute(x, axes, [(i, i ^ mask) for i in range(size)])


def exchange(x, axes):
    got = [swap(x, axes, mask) for mask in reversed(range(1, lax.axis_size(axes)))]
    return [x] + got[::-1]


def tree_sum(got):
    while len(got) > 1:
        got = [got[i] + got[i + 1] for i in range(0, len(got), 2)]
    return got[0]


def pairwise_sum(x, axes):
    mask = 1
    while mask < lax.axis_size(axes):
        x = x + swap(x, axes, mask)
        mask *= 2
    return x


def tie(*xs):
    return lax.optimization_barrier(xs)


def params_of(mib):
    return pltpu.CompilerParams(vmem_limit_bytes=mib * 1024 * 1024)


def step_kernel(takes, finishes, b, sends, starts, brings, carries, *refs):
    refs = list(refs[1:])
    take = lambda yes: refs.pop(0) if yes else None
    got = [take(takes or finishes) for _ in range(2)]
    mine = take(finishes)
    direct = [take(sends) for _ in range(2)]
    relay = [take(sends) for _ in range(2)]
    onward = take(starts)
    first = b == 0
    again = finishes and not first
    cols_in, rows_in, _ = take(again), take(again), take(again)
    stats_in = take(brings is not None or carries is not None)
    out = [take(sends or starts) for _ in range(2)]
    cols_out, rows_out, summed_out = take(finishes), take(finishes), take(finishes)
    stats_out = take(brings is not None)
    row_parts = take(finishes)
    t = pl.program_id(0)
    tile, width = (onward if starts else mine if finishes else direct[0]).shape[-2:]
    part = tile * pl.num_programs(0)

    def rows_of(slot):
        return pl.ds(pl.multiple_of(slot * part + t * tile, sublanes), tile)

    @pl.when(t == 0)
    def _():
        if finishes:
            cols_out[...] = jnp.zeros_like(cols_out) if first else cols_in[...]
            rows_out[...] = jnp.zeros_like(rows_out) if first else rows_in[...]
        if brings is not None:
            brought = got[brings][got[brings].shape[0] - sublanes :, : stats_in.shape[1]]
            stats_out[...] = stats_in[...] + brought
        if carries is not None:
            stats = stats_in if brings is None else stats_out
            out[carries][out[carries].shape[0] - sublanes :, : stats.shape[1]] = stats[...]

    for half in range(2):
        if starts:
            out[half][rows_of(2 if sends else 0)] = onward[half].astype(f32)
        if sends:
            out[half][rows_of(0)] = direct[half][...].astype(f32)
            passed = got[half][rows_of(2 if finishes else 0)]
            out[1 - half][rows_of(1)] = passed + relay[half][...].astype(f32)
        if finishes:
            total = mine[half].astype(f32) + got[half][rows_of(0)] + got[1 - half][rows_of(1)]
            summed_out[half] = total
            squares = total * total
            row_parts[rows_of(half)] = sum(squares[:, i : i + lanes] for i in range(0, width, lanes))
            cols_out[...] += sum(squares[i : i + sublanes] for i in range(0, tile, sublanes))

    if finishes:

        @pl.when(t == pl.num_programs(0) - 1)
        def _():
            along = lax.dot_general(
                jnp.ones((sublanes, lanes), f32),
                row_parts[...],
                (((1,), (1,)), ((), ())),
                precision=lax.Precision.HIGHEST,
                preferred_element_type=f32,
            )
            rows_out[b : b + 1] = along[0:1]


def step(j, total_blocks, me, partials, got, sums, stats, brings, carries):
    mats, _, count, _, part, width = partials.shape
    finishes = j >= 2
    takes = 0 <= j < total_blocks
    tile = min(tile_rows if takes else 2 * tile_rows, part)
    sends = takes
    starts = j + 2 < total_blocks
    b = (j - 2) % count
    first = finishes and b == 0

    def piece_spec(block, mask, half):
        m, b = divmod(block, count)
        if half is None:
            return pl.BlockSpec(
                (None, None, None, 2, tile, width),
                lambda t, at: (m, at[0] ^ mask, b, 0, t, 0),
            )
        return pl.BlockSpec(
            (None, None, None, None, tile, width),
            lambda t, at: (m, at[0] ^ mask, b, half, t, 0),
        )

    in_vmem = pl.BlockSpec(memory_space=pltpu.VMEM)
    operands, in_specs = [], []

    def add(x, spec):
        operands.append(x)
        in_specs.append(spec)

    if j >= 0:
        for x in got:
            add(x, in_vmem)
    if finishes:
        add(partials, piece_spec(j - 2, 0, None))
    if sends:
        for half, mask in ((0, 1), (1, 2)):
            add(partials, piece_spec(j, mask, half))
        for half, mask in ((0, 2), (1, 1)):
            add(partials, piece_spec(j, mask, half))
    if starts:
        add(partials, piece_spec(j + 2, 3, None))

    slots = (2 if sends else 0) + (1 if starts else 0)
    out_shape, out_specs, scratch, aliases = [], [], [], {}
    if slots:
        for link in range(2):
            size = slots * part + (sublanes if link == carries else 0)
            out_shape.append(jax.ShapeDtypeStruct((size, width), f32))
            out_specs.append(in_vmem)
    whole = lambda *shape: pl.BlockSpec(shape, lambda t, at: (0,) * len(shape))
    if finishes:
        rows_shape = (count, 2 * part)
        if not first:
            add(sums[0], whole(sublanes, width))
            add(sums[1], whole(*rows_shape))
            aliases[1 + len(operands)] = len(out_shape) + 2
            add(sums[2], pl.BlockSpec(memory_space=pl.ANY))
        out_shape.append(jax.ShapeDtypeStruct((sublanes, width), f32))
        out_specs.append(whole(sublanes, width))
        out_shape.append(jax.ShapeDtypeStruct(rows_shape, f32))
        out_specs.append(whole(*rows_shape))
        out_shape.append(jax.ShapeDtypeStruct((count, 2, part, width), f32))
        out_specs.append(pl.BlockSpec((None, 2, tile, width), lambda t, at: (b, 0, t, 0)))
        scratch.append(pltpu.VMEM((2 * part, lanes), f32))
    if brings is not None or carries is not None:
        add(stats, whole(*stats.shape))
    if brings is not None:
        out_shape.append(jax.ShapeDtypeStruct(stats.shape, f32))
        out_specs.append(whole(*stats.shape))
    moved = part * width * (4 * (2 * slots + 8) + 2 * 8)
    result = pl.pallas_call(
        functools.partial(step_kernel, takes, finishes, b, sends, starts, brings, carries),
        out_shape=out_shape,
        grid_spec=pltpu.PrefetchScalarGridSpec(
            num_scalar_prefetch=1,
            grid=(part // tile,),
            in_specs=in_specs,
            out_specs=out_specs,
            scratch_shapes=scratch,
        ),
        input_output_aliases=aliases,
        compiler_params=params_of(34),
        cost_estimate=pl.CostEstimate(
            flops=part * width * 20, bytes_accessed=moved, transcendentals=0
        ),
        name="step",
    )(me, *operands)
    sent = list(result[:2]) if slots else None
    rest = list(result[2:] if slots else result)
    return sent, rest[:3] if finishes else None, rest[3] if brings is not None else stats


def weighted_kernel(extent, factor, cols, summed, *refs):
    *totals, rows_out, stats, weighted = refs
    count, _, part, width = summed.shape
    total = tree_sum([x[...] for x in totals])
    row_new = decay_rate * factor[...] + (1.0 - decay_rate) * (total / extent + tiny_eps)
    rows_out[...] = row_new
    inverse = jnp.transpose(1.0 / row_new)
    weighted[...] = jnp.zeros_like(weighted)
    for i in range(count):
        for r in range(0, 2 * part, sublanes):
            half, at = divmod(r, part)
            x = summed[i, half, at : at + sublanes]
            weighted[...] += x * x * inverse[r : r + sublanes, i : i + 1]
    size = width // sublanes
    for at, x in ((0, cols), (size, weighted)):
        sums = jnp.sum(x[...], axis=0, keepdims=True)
        for k in range(sublanes):
            stats[k : k + 1, at : at + size] = sums[:, k * size : (k + 1) * size]
    level = jnp.sum(jnp.sum(row_new, axis=0, keepdims=True), axis=1, keepdims=True)
    stats[:, 2 * size :] = jnp.broadcast_to(level, (sublanes, lanes))


def weighted_sums(extent, totals, factor, cols, summed):
    width = summed.shape[-1]
    in_vmem = pl.BlockSpec(memory_space=pltpu.VMEM)
    return pl.pallas_call(
        functools.partial(weighted_kernel, extent),
        in_specs=[in_vmem] * (3 + len(totals)),
        out_specs=[in_vmem] * 2,
        out_shape=[
            jax.ShapeDtypeStruct(totals[0].shape, f32),
            jax.ShapeDtypeStruct((sublanes, 2 * width // sublanes + lanes), f32),
        ],
        scratch_shapes=[pltpu.VMEM((sublanes, width), f32)],
        compiler_params=params_of(16),
        cost_estimate=pl.CostEstimate(
            flops=3 * summed.size, bytes_accessed=4 * summed.size, transcendentals=0
        ),
        name="weighted",
    )(factor.reshape(totals[0].shape), cols, summed, *totals)


def column_kernel(extent, factor, *refs):
    *parts, cols_out, pair, sums = refs
    stats = tree_sum([x[...] for x in parts])
    size = factor.shape[1] // sublanes
    for i in range(2):
        for k in range(sublanes):
            sums[i : i + 1, k * size : (k + 1) * size] = stats[k : k + 1, i * size : (i + 1) * size]
    col_new = decay_rate * factor[...] + (1.0 - decay_rate) * (sums[0:1] / extent + tiny_eps)
    cols_out[...] = col_new
    total = jnp.sum(sums[1:2] / col_new, axis=1, keepdims=True)
    pair[...] = stats[:, 2 * size :] / extent
    pair[0:1] = jnp.broadcast_to(total, (1, lanes))


def column_stage(extent, factor, parts):
    return pl.pallas_call(
        functools.partial(column_kernel, extent),
        in_specs=[pl.BlockSpec(memory_space=pltpu.VMEM)] * (1 + len(parts)),
        out_specs=[pl.BlockSpec(memory_space=pltpu.VMEM)] * 2,
        out_shape=[
            jax.ShapeDtypeStruct(factor.shape, f32),
            jax.ShapeDtypeStruct((sublanes, lanes), f32),
        ],
        scratch_shapes=[pltpu.VMEM((sublanes, factor.shape[1]), f32)],
        compiler_params=params_of(4),
        name="column",
    )(factor, *parts)


def finish_kernel(m, extent, partners, staged, row_new, col_new, summed, params, *refs):
    pairs, (new_params, update, column, by_col) = refs[:partners], refs[-4:]
    count, _, part, width = summed.shape

    def scale():
        row_level = pairs[0][1:2, 0:1]
        total = tree_sum([x[0:1, 0:1] for x in pairs]) * row_level
        spread = jnp.sqrt(total / (extent * extent))
        factor = jnp.sqrt(row_level) / jnp.maximum(1.0, spread / clip_limit)
        by_row = jnp.transpose(lax.rsqrt(row_new[...]) * factor)
        for i in range(count):
            column[i] = jnp.broadcast_to(by_row[:, i : i + 1], column.shape[1:])
        by_col[...] = lax.rsqrt(col_new[...])

    def body(*blocks):
        new_p, moved = blocks[-2:]
        i = pl.program_id(0)
        pl.when(i == 0)(scale)
        for half in range(2):
            for r in range(0, part, sublanes):
                at = half * part + r
                mine = column[i, at : at + sublanes][:, 0:1]
                y = summed[i, half, r : r + sublanes] * mine * by_col[...]
                moved[half, r : r + sublanes] = y
                p = params[i, half, r : r + sublanes] if staged else blocks[0][half, r : r + sublanes]
                new_p[half, r : r + sublanes] = p - learn_rate * y

    of_matrix = pl.BlockSpec((None, None, 2, part, width), lambda i: (m, i, 0, 0, 0))
    pltpu.emit_pipeline(
        body, grid=(count,), in_specs=[] if staged else [of_matrix], out_specs=[of_matrix] * 2
    )(*([] if staged else [params]), new_params, update)


def finish(m, extent, row_new, col_new, pairs, summed, params, outs, mib):
    count, _, part, width = summed.shape
    held = () if outs is None else outs
    staged = params.ndim == summed.ndim
    in_hbm = pl.BlockSpec(memory_space=pltpu.HBM)
    in_vmem = pl.BlockSpec(memory_space=pltpu.VMEM)
    return pl.pallas_call(
        functools.partial(finish_kernel, m, extent, len(pairs), staged),
        in_specs=[in_vmem] * 3
        + [in_vmem if staged else in_hbm]
        + [in_vmem] * len(pairs)
        + [in_hbm] * len(held),
        out_specs=[in_hbm] * 2,
        out_shape=[jax.ShapeDtypeStruct(held[0].shape if staged else params.shape, f32)] * 2,
        scratch_shapes=[
            pltpu.VMEM((count, 2 * part, lanes), f32),
            pltpu.VMEM((1, width), f32),
        ],
        input_output_aliases={4 + len(pairs) + i: i for i in range(len(held))},
        compiler_params=params_of(mib),
        cost_estimate=pl.CostEstimate(
            flops=4 * summed.size, bytes_accessed=16 * summed.size, transcendentals=0
        ),
        name="finish",
    )(row_new, col_new, summed, params, *pairs, *held)


def per_device(partials, params, row_factor, col_factor):
    mats, rows, block_cols = params.shape
    extent = block_cols * lax.axis_size("col")
    me = lax.axis_index("dp").astype(jnp.int32).reshape(1)
    count = blocks_of_matrix
    part = rows // (2 * count)
    total_blocks = mats * count
    pieces = partials.reshape(mats, partials.shape[2], count, 2, part, block_cols)
    blocked = params.reshape(mats, count, 2, part, block_cols)
    new_rows, new_columns = [], []

    def row_stage(m, sums):
        cols, rows_along, summed = sums
        row_new, stats = weighted_sums(
            extent, exchange(rows_along, "col"), row_factor[m], cols, summed
        )
        new_rows.append(row_new.reshape(rows))
        return row_new, pairwise_sum(stats, "row")

    def col_stage(m, parts):
        col_new, pair = column_stage(extent, col_factor[m : m + 1], parts)
        new_columns.append(col_new)
        return col_new, exchange(pair, "col")

    flying = {}
    sums = stats = outs = None
    last = {}
    for j in range(-2, total_blocks + 2):
        m, b = divmod(j - 2, count)
        since = b + 1 if m >= 1 else None
        carries = {1: 0, 3: 1}.get(since)
        brings = {3: 0, 5: 1}.get(since)
        got = flying.pop(j, None)
        sent, sums, stats = step(
            j, total_blocks, me, pieces, got, sums, stats, brings, carries
        )
        if sent is not None:
            flying[j + 2] = [swap(sent[0], "dp", 1), swap(sent[1], "dp", 2)]
        if sums:
            me, *sums = tie(me, *sums)
        else:
            me, *_ = tie(me, *sent)
        if 0 <= m < mats - 1 and b == count - 1:
            row_new, stats = row_stage(m, sums)
            last = dict(m=m, row_new=row_new, summed=sums[2])
            me, stats = tie(me, stats)
        if since == 5:
            stats, me = tie(stats, me)
            col_new, pairs = col_stage(last["m"], [stats])
            outs = finish(
                last["m"], extent, last["row_new"], col_new, pairs, last["summed"], blocked, outs, 36
            )
            me, *outs = tie(me, *outs)
        if j == total_blocks - 1:
            me, last_params = tie(me, blocked[mats - 1])
    row_new, stats = row_stage(mats - 1, sums)
    col_new, pairs = col_stage(mats - 1, exchange(stats, "dp"))
    new_params, update = finish(
        mats - 1, extent, row_new, col_new, pairs, sums[2], last_params, outs, 12
    )
    return (
        new_params.reshape(params.shape),
        update.reshape(params.shape),
        jnp.stack(new_rows),
        jnp.concatenate(new_columns, axis=0),
    )


def solution(mesh):
    placed = (
        P("dp", None, None, "row", None, "col"),
        P(None, ("dp", "row"), "col"),
        P(None, ("dp", "row")),
        P(None, "col"),
    )
    return jax.shard_map(
        per_device,
        mesh=mesh,
        in_specs=placed,
        out_specs=(
            P(None, ("dp", "row"), "col"),
            P(None, ("dp", "row"), "col"),
            P(None, ("dp", "row")),
            P(None, "col"),
        ),
        check_vma=False,
    )
```

```python
import functools

import jax
import jax.numpy as jnp
from jax import lax
from jax.experimental import pallas as pl
from jax.experimental.pallas import tpu as pltpu
from jax.sharding import PartitionSpec as P

decay_rate = 1.0 - 2.0 ** (-0.8)
tiny_eps = 1e-30
clip_limit = 1.0
learn_rate = 0.01

lanes = 128
sublanes = 8
blocks_of_matrix = 8
tile_rows = 16
f32 = jnp.float32


def swap(x, axes, mask):
    size = lax.axis_size(axes)
    return lax.ppermute(x, axes, [(i, i ^ mask) for i in range(size)])


def exchange(x, axes):
    got = [swap(x, axes, mask) for mask in reversed(range(1, lax.axis_size(axes)))]
    return [x] + got[::-1]


def tree_sum(got):
    while len(got) > 1:
        got = [got[i] + got[i + 1] for i in range(0, len(got), 2)]
    return got[0]


def pairwise_sum(x, axes):
    mask = 1
    while mask < lax.axis_size(axes):
        x = x + swap(x, axes, mask)
        mask *= 2
    return x


def tie(*xs):
    return lax.optimization_barrier(xs)


def params_of(mib):
    return pltpu.CompilerParams(vmem_limit_bytes=mib * 1024 * 1024)


def step_kernel(takes, finishes, b, sends, starts, brings, carries, *refs):
    refs = list(refs[1:])
    take = lambda yes: refs.pop(0) if yes else None
    got = [take(takes or finishes) for _ in range(2)]
    mine = take(finishes)
    direct = [take(sends) for _ in range(2)]
    relay = [take(sends) for _ in range(2)]
    onward = take(starts)
    first = b == 0
    again = finishes and not first
    cols_in, rows_in, _ = take(again), take(again), take(again)
    stats_in = take(brings is not None or carries is not None)
    out = [take(sends or starts) for _ in range(2)]
    cols_out, rows_out, summed_out = take(finishes), take(finishes), take(finishes)
    stats_out = take(brings is not None)
    row_parts = take(finishes)
    t = pl.program_id(0)
    tile, width = (onward if starts else mine if finishes else direct[0]).shape[-2:]
    part = tile * pl.num_programs(0)

    def rows_of(slot):
        return pl.ds(pl.multiple_of(slot * part + t * tile, sublanes), tile)

    @pl.when(t == 0)
    def _():
        if finishes:
            cols_out[...] = jnp.zeros_like(cols_out) if first else cols_in[...]
            rows_out[...] = jnp.zeros_like(rows_out) if first else rows_in[...]
        if brings is not None:
            brought = got[brings][got[brings].shape[0] - sublanes :, : stats_in.shape[1]]
            stats_out[...] = stats_in[...] + brought
        if carries is not None:
            stats = stats_in if brings is None else stats_out
            out[carries][out[carries].shape[0] - sublanes :, : stats.shape[1]] = stats[...]

    for half in range(2):
        if starts:
            out[half][rows_of(2 if sends else 0)] = onward[half].astype(f32)
        if sends:
            out[half][rows_of(0)] = direct[half][...].astype(f32)
            passed = got[half][rows_of(2 if finishes else 0)]
            out[1 - half][rows_of(1)] = passed + relay[half][...].astype(f32)
        if finishes:
            total = mine[half].astype(f32) + got[half][rows_of(0)] + got[1 - half][rows_of(1)]
            summed_out[half] = total
            squares = total * total
            row_parts[rows_of(half)] = sum(squares[:, i : i + lanes] for i in range(0, width, lanes))
            cols_out[...] += sum(squares[i : i + sublanes] for i in range(0, tile, sublanes))

    if finishes:

        @pl.when(t == pl.num_programs(0) - 1)
        def _():
            along = lax.dot_general(
                jnp.ones((sublanes, lanes), f32),
                row_parts[...],
                (((1,), (1,)), ((), ())),
                precision=lax.Precision.HIGHEST,
                preferred_element_type=f32,
            )
            rows_out[b : b + 1] = along[0:1]


def step(j, total_blocks, me, partials, got, sums, stats, brings, carries):
    mats, _, count, _, part, width = partials.shape
    finishes = j >= 2
    takes = 0 <= j < total_blocks
    tile = min(tile_rows if takes else 2 * tile_rows, part)
    sends = takes
    starts = j + 2 < total_blocks
    b = (j - 2) % count
    first = finishes and b == 0

    def piece_spec(block, mask, half):
        m, b = divmod(block, count)
        if half is None:
            return pl.BlockSpec(
                (None, None, None, 2, tile, width),
                lambda t, at: (m, at[0] ^ mask, b, 0, t, 0),
            )
        return pl.BlockSpec(
            (None, None, None, None, tile, width),
            lambda t, at: (m, at[0] ^ mask, b, half, t, 0),
        )

    in_vmem = pl.BlockSpec(memory_space=pltpu.VMEM)
    operands, in_specs = [], []

    def add(x, spec):
        operands.append(x)
        in_specs.append(spec)

    if j >= 0:
        for x in got:
            add(x, in_vmem)
    if finishes:
        add(partials, piece_spec(j - 2, 0, None))
    if sends:
        for half, mask in ((0, 1), (1, 2)):
            add(partials, piece_spec(j, mask, half))
        for half, mask in ((0, 2), (1, 1)):
            add(partials, piece_spec(j, mask, half))
    if starts:
        add(partials, piece_spec(j + 2, 3, None))

    slots = (2 if sends else 0) + (1 if starts else 0)
    out_shape, out_specs, scratch, aliases = [], [], [], {}
    if slots:
        for link in range(2):
            size = slots * part + (sublanes if link == carries else 0)
            out_shape.append(jax.ShapeDtypeStruct((size, width), f32))
            out_specs.append(in_vmem)
    whole = lambda *shape: pl.BlockSpec(shape, lambda t, at: (0,) * len(shape))
    if finishes:
        rows_shape = (count, 2 * part)
        if not first:
            add(sums[0], whole(sublanes, width))
            add(sums[1], whole(*rows_shape))
            aliases[1 + len(operands)] = len(out_shape) + 2
            add(sums[2], pl.BlockSpec(memory_space=pl.ANY))
        out_shape.append(jax.ShapeDtypeStruct((sublanes, width), f32))
        out_specs.append(whole(sublanes, width))
        out_shape.append(jax.ShapeDtypeStruct(rows_shape, f32))
        out_specs.append(whole(*rows_shape))
        out_shape.append(jax.ShapeDtypeStruct((count, 2, part, width), f32))
        out_specs.append(pl.BlockSpec((None, 2, tile, width), lambda t, at: (b, 0, t, 0)))
        scratch.append(pltpu.VMEM((2 * part, lanes), f32))
    if brings is not None or carries is not None:
        add(stats, whole(*stats.shape))
    if brings is not None:
        out_shape.append(jax.ShapeDtypeStruct(stats.shape, f32))
        out_specs.append(whole(*stats.shape))
    moved = part * width * (4 * (2 * slots + 8) + 2 * 8)
    result = pl.pallas_call(
        functools.partial(step_kernel, takes, finishes, b, sends, starts, brings, carries),
        out_shape=out_shape,
        grid_spec=pltpu.PrefetchScalarGridSpec(
            num_scalar_prefetch=1,
            grid=(part // tile,),
            in_specs=in_specs,
            out_specs=out_specs,
            scratch_shapes=scratch,
        ),
        input_output_aliases=aliases,
        compiler_params=params_of(34),
        cost_estimate=pl.CostEstimate(
            flops=part * width * 20, bytes_accessed=moved, transcendentals=0
        ),
        name="step",
    )(me, *operands)
    sent = list(result[:2]) if slots else None
    rest = list(result[2:] if slots else result)
    return sent, rest[:3] if finishes else None, rest[3] if brings is not None else stats


def weighted_kernel(extent, factor, cols, summed, *refs):
    *totals, rows_out, stats, weighted = refs
    count, _, part, width = summed.shape
    total = tree_sum([x[...] for x in totals])
    row_new = decay_rate * factor[...] + (1.0 - decay_rate) * (total / extent + tiny_eps)
    rows_out[...] = row_new
    inverse = jnp.transpose(1.0 / row_new)
    weighted[...] = jnp.zeros_like(weighted)
    for i in range(count):
        for r in range(0, 2 * part, sublanes):
            half, at = divmod(r, part)
            x = summed[i, half, at : at + sublanes]
            weighted[...] += x * x * inverse[r : r + sublanes, i : i + 1]
    size = width // sublanes
    for at, x in ((0, cols), (size, weighted)):
        sums = jnp.sum(x[...], axis=0, keepdims=True)
        for k in range(sublanes):
            stats[k : k + 1, at : at + size] = sums[:, k * size : (k + 1) * size]
    level = jnp.sum(jnp.sum(row_new, axis=0, keepdims=True), axis=1, keepdims=True)
    stats[:, 2 * size :] = jnp.broadcast_to(level, (sublanes, lanes))


def weighted_sums(extent, totals, factor, cols, summed):
    width = summed.shape[-1]
    in_vmem = pl.BlockSpec(memory_space=pltpu.VMEM)
    return pl.pallas_call(
        functools.partial(weighted_kernel, extent),
        in_specs=[in_vmem] * (3 + len(totals)),
        out_specs=[in_vmem] * 2,
        out_shape=[
            jax.ShapeDtypeStruct(totals[0].shape, f32),
            jax.ShapeDtypeStruct((sublanes, 2 * width // sublanes + lanes), f32),
        ],
        scratch_shapes=[pltpu.VMEM((sublanes, width), f32)],
        compiler_params=params_of(16),
        cost_estimate=pl.CostEstimate(
            flops=3 * summed.size, bytes_accessed=4 * summed.size, transcendentals=0
        ),
        name="weighted",
    )(factor.reshape(totals[0].shape), cols, summed, *totals)


def column_kernel(extent, factor, *refs):
    *parts, cols_out, pair, sums = refs
    stats = tree_sum([x[...] for x in parts])
    size = factor.shape[1] // sublanes
    for i in range(2):
        for k in range(sublanes):
            sums[i : i + 1, k * size : (k + 1) * size] = stats[k : k + 1, i * size : (i + 1) * size]
    col_new = decay_rate * factor[...] + (1.0 - decay_rate) * (sums[0:1] / extent + tiny_eps)
    cols_out[...] = col_new
    total = jnp.sum(sums[1:2] / col_new, axis=1, keepdims=True)
    pair[...] = stats[:, 2 * size :] / extent
    pair[0:1] = jnp.broadcast_to(total, (1, lanes))


def column_stage(extent, factor, parts):
    return pl.pallas_call(
        functools.partial(column_kernel, extent),
        in_specs=[pl.BlockSpec(memory_space=pltpu.VMEM)] * (1 + len(parts)),
        out_specs=[pl.BlockSpec(memory_space=pltpu.VMEM)] * 2,
        out_shape=[
            jax.ShapeDtypeStruct(factor.shape, f32),
            jax.ShapeDtypeStruct((sublanes, lanes), f32),
        ],
        scratch_shapes=[pltpu.VMEM((sublanes, factor.shape[1]), f32)],
        compiler_params=params_of(4),
        name="column",
    )(factor, *parts)


def finish_kernel(m, extent, partners, staged, row_new, col_new, summed, params, *refs):
    pairs, (new_params, update, column, by_col) = refs[:partners], refs[-4:]
    count, _, part, width = summed.shape

    def scale():
        row_level = pairs[0][1:2, 0:1]
        total = tree_sum([x[0:1, 0:1] for x in pairs]) * row_level
        spread = jnp.sqrt(total / (extent * extent))
        factor = jnp.sqrt(row_level) / jnp.maximum(1.0, spread / clip_limit)
        by_row = jnp.transpose(lax.rsqrt(row_new[...]) * factor)
        for i in range(count):
            column[i] = jnp.broadcast_to(by_row[:, i : i + 1], column.shape[1:])
        by_col[...] = lax.rsqrt(col_new[...])

    def body(*blocks):
        new_p, moved = blocks[-2:]
        i, half = pl.program_id(0), pl.program_id(1)
        pl.when((i == 0) & (half == 0))(scale)
        for r in range(0, part, sublanes):
            rows = slice(r, r + sublanes)
            at = pl.ds(pl.multiple_of(half * part + r, sublanes), sublanes)
            y = summed[i, half, rows] * column[i, at][:, 0:1] * by_col[...]
            moved[rows] = y
            new_p[rows] = (params[i, half, rows] if staged else blocks[0][rows]) - learn_rate * y

    of_matrix = pl.BlockSpec((None, None, None, part, width), lambda i, h: (m, i, h, 0, 0))
    pltpu.emit_pipeline(
        body, grid=(count, 2), in_specs=[] if staged else [of_matrix], out_specs=[of_matrix] * 2
    )(*([] if staged else [params]), new_params, update)


def finish(m, extent, row_new, col_new, pairs, summed, params, outs, mib):
    count, _, part, width = summed.shape
    held = () if outs is None else outs
    staged = params.ndim == summed.ndim
    in_hbm = pl.BlockSpec(memory_space=pltpu.HBM)
    in_vmem = pl.BlockSpec(memory_space=pltpu.VMEM)
    return pl.pallas_call(
        functools.partial(finish_kernel, m, extent, len(pairs), staged),
        in_specs=[in_vmem] * 3
        + [in_vmem if staged else in_hbm]
        + [in_vmem] * len(pairs)
        + [in_hbm] * len(held),
        out_specs=[in_hbm] * 2,
        out_shape=[jax.ShapeDtypeStruct(held[0].shape if staged else params.shape, f32)] * 2,
        scratch_shapes=[
            pltpu.VMEM((count, 2 * part, lanes), f32),
            pltpu.VMEM((1, width), f32),
        ],
        input_output_aliases={4 + len(pairs) + i: i for i in range(len(held))},
        compiler_params=params_of(mib),
        cost_estimate=pl.CostEstimate(
            flops=4 * summed.size, bytes_accessed=16 * summed.size, transcendentals=0
        ),
        name="finish",
    )(row_new, col_new, summed, params, *pairs, *held)


def per_device(partials, params, row_factor, col_factor):
    mats, rows, block_cols = params.shape
    extent = block_cols * lax.axis_size("col")
    me = lax.axis_index("dp").astype(jnp.int32).reshape(1)
    count = blocks_of_matrix
    part = rows // (2 * count)
    total_blocks = mats * count
    pieces = partials.reshape(mats, partials.shape[2], count, 2, part, block_cols)
    blocked = params.reshape(mats, count, 2, part, block_cols)
    new_rows, new_columns = [], []

    def row_stage(m, sums):
        cols, rows_along, summed = sums
        row_new, stats = weighted_sums(
            extent, [pairwise_sum(rows_along, "col")], row_factor[m], cols, summed
        )
        new_rows.append(row_new.reshape(rows))
        return row_new, pairwise_sum(stats, "row")

    def col_stage(m, parts):
        col_new, pair = column_stage(extent, col_factor[m : m + 1], parts)
        new_columns.append(col_new)
        return col_new, exchange(pair, "col")

    flying = {}
    sums = stats = outs = None
    last = {}
    for j in range(-2, total_blocks + 2):
        m, b = divmod(j - 2, count)
        since = b + 1 if m >= 1 else None
        carries = {1: 0, 3: 1}.get(since)
        brings = {3: 0, 5: 1}.get(since)
        got = flying.pop(j, None)
        sent, sums, stats = step(
            j, total_blocks, me, pieces, got, sums, stats, brings, carries
        )
        if sent is not None:
            flying[j + 2] = [swap(sent[0], "dp", 1), swap(sent[1], "dp", 2)]
        if sums:
            me, *sums = tie(me, *sums)
        else:
            me, *_ = tie(me, *sent)
        if 0 <= m < mats - 1 and b == count - 1:
            row_new, stats = row_stage(m, sums)
            last = dict(m=m, row_new=row_new, summed=sums[2])
            me, stats = tie(me, stats)
        if since == 5:
            stats, me = tie(stats, me)
            col_new, pairs = col_stage(last["m"], [stats])
            outs = finish(
                last["m"], extent, last["row_new"], col_new, pairs, last["summed"], blocked, outs, 36
            )
            me, *outs = tie(me, *outs)
        if j == total_blocks - 1:
            me, last_params = tie(me, blocked[mats - 1])
    row_new, stats = row_stage(mats - 1, sums)
    col_new, pairs = col_stage(mats - 1, exchange(stats, "dp"))
    new_params, update = finish(
        mats - 1, extent, row_new, col_new, pairs, sums[2], last_params, outs, 12
    )
    return (
        new_params.reshape(params.shape),
        update.reshape(params.shape),
        jnp.stack(new_rows),
        jnp.concatenate(new_columns, axis=0),
    )


def solution(mesh):
    placed = (
        P("dp", None, None, "row", None, "col"),
        P(None, ("dp", "row"), "col"),
        P(None, ("dp", "row")),
        P(None, "col"),
    )
    return jax.shard_map(
        per_device,
        mesh=mesh,
        in_specs=placed,
        out_specs=(
            P(None, ("dp", "row"), "col"),
            P(None, ("dp", "row"), "col"),
            P(None, ("dp", "row")),
            P(None, "col"),
        ),
        check_vma=False,
    )
```

```python
import functools
import itertools

import jax
import jax.numpy as jnp
from jax import lax
from jax.experimental import pallas as pl
from jax.experimental.pallas import tpu as pltpu
from jax.sharding import PartitionSpec as P

decay_rate = 1.0 - 2.0 ** (-0.8)
tiny_eps = 1e-30
clip_limit = 1.0
learn_rate = 0.01

lanes = 128
sublanes = 8
blocks_of_matrix = 8
tile_rows = 16
f32 = jnp.float32


def swap(x, axes, mask):
    size = lax.axis_size(axes)
    return lax.ppermute(x, axes, [(i, i ^ mask) for i in range(size)])


def exchange(x, axes):
    got = [swap(x, axes, mask) for mask in reversed(range(1, lax.axis_size(axes)))]
    return [x] + got[::-1]


def tree_sum(got):
    while len(got) > 1:
        got = [got[i] + got[i + 1] for i in range(0, len(got), 2)]
    return got[0]


def pairwise_sum(x, axes):
    mask = 1
    while mask < lax.axis_size(axes):
        x = x + swap(x, axes, mask)
        mask *= 2
    return x


def tie(*xs):
    return lax.optimization_barrier(xs)


def params_of(mib):
    return pltpu.CompilerParams(vmem_limit_bytes=mib * 1024 * 1024)


def step_kernel(takes, finishes, b, sends, starts, brings, carries, *refs):
    refs = list(refs[1:])
    take = lambda yes: refs.pop(0) if yes else None
    got = [take(takes or finishes) for _ in range(2)]
    mine = take(finishes)
    direct = [take(sends) for _ in range(2)]
    relay = [take(sends) for _ in range(2)]
    onward = take(starts)
    first = b == 0
    again = finishes and not first
    cols_in, rows_in, _ = take(again), take(again), take(again)
    stats_in = take(brings is not None or carries is not None)
    out = [take(sends or starts) for _ in range(2)]
    cols_out, rows_out, summed_out = take(finishes), take(finishes), take(finishes)
    stats_out = take(brings is not None)
    row_parts = take(finishes)
    t = pl.program_id(0)
    tile, width = (onward if starts else mine if finishes else direct[0]).shape[-2:]
    part = tile * pl.num_programs(0)

    def rows_of(slot):
        return pl.ds(pl.multiple_of(slot * part + t * tile, sublanes), tile)

    @pl.when(t == 0)
    def _():
        if finishes:
            cols_out[...] = jnp.zeros_like(cols_out) if first else cols_in[...]
            rows_out[...] = jnp.zeros_like(rows_out) if first else rows_in[...]
        if brings is not None:
            brought = got[brings][got[brings].shape[0] - sublanes :, : stats_in.shape[1]]
            stats_out[...] = stats_in[...] + brought
        if carries is not None:
            stats = stats_in if brings is None else stats_out
            out[carries][out[carries].shape[0] - sublanes :, : stats.shape[1]] = stats[...]

    for half in range(2):
        if starts:
            out[half][rows_of(2 if sends else 0)] = onward[half].astype(f32)
        if sends:
            out[half][rows_of(0)] = direct[half][...].astype(f32)
            passed = got[half][rows_of(2 if finishes else 0)]
            out[1 - half][rows_of(1)] = passed + relay[half][...].astype(f32)
        if finishes:
            total = mine[half].astype(f32) + got[half][rows_of(0)] + got[1 - half][rows_of(1)]
            summed_out[half] = total
            squares = total * total
            row_parts[rows_of(half)] = sum(squares[:, i : i + lanes] for i in range(0, width, lanes))
            cols_out[...] += sum(squares[i : i + sublanes] for i in range(0, tile, sublanes))

    if finishes:

        @pl.when(t == pl.num_programs(0) - 1)
        def _():
            along = lax.dot_general(
                jnp.ones((sublanes, lanes), f32),
                row_parts[...],
                (((1,), (1,)), ((), ())),
                precision=lax.Precision.HIGHEST,
                preferred_element_type=f32,
            )
            rows_out[b : b + 1] = along[0:1]


def step(j, total_blocks, me, partials, got, sums, stats, brings, carries):
    mats, _, count, _, part, width = partials.shape
    finishes = j >= 2
    takes = 0 <= j < total_blocks
    tile = min(tile_rows if takes else 2 * tile_rows, part)
    sends = takes
    starts = j + 2 < total_blocks
    b = (j - 2) % count
    first = finishes and b == 0

    def piece_spec(block, mask, half):
        m, b = divmod(block, count)
        if half is None:
            return pl.BlockSpec(
                (None, None, None, 2, tile, width),
                lambda t, at: (m, at[0] ^ mask, b, 0, t, 0),
            )
        return pl.BlockSpec(
            (None, None, None, None, tile, width),
            lambda t, at: (m, at[0] ^ mask, b, half, t, 0),
        )

    in_vmem = pl.BlockSpec(memory_space=pltpu.VMEM)
    operands, in_specs = [], []

    def add(x, spec):
        operands.append(x)
        in_specs.append(spec)

    if j >= 0:
        for x in got:
            add(x, in_vmem)
    if finishes:
        add(partials, piece_spec(j - 2, 0, None))
    if sends:
        for half, mask in ((0, 1), (1, 2)):
            add(partials, piece_spec(j, mask, half))
        for half, mask in ((0, 2), (1, 1)):
            add(partials, piece_spec(j, mask, half))
    if starts:
        add(partials, piece_spec(j + 2, 3, None))

    slots = (2 if sends else 0) + (1 if starts else 0)
    out_shape, out_specs, scratch, aliases = [], [], [], {}
    if slots:
        for link in range(2):
            size = slots * part + (sublanes if link == carries else 0)
            out_shape.append(jax.ShapeDtypeStruct((size, width), f32))
            out_specs.append(in_vmem)
    whole = lambda *shape: pl.BlockSpec(shape, lambda t, at: (0,) * len(shape))
    if finishes:
        rows_shape = (count, 2 * part)
        if not first:
            add(sums[0], whole(sublanes, width))
            add(sums[1], whole(*rows_shape))
            aliases[1 + len(operands)] = len(out_shape) + 2
            add(sums[2], pl.BlockSpec(memory_space=pl.ANY))
        out_shape.append(jax.ShapeDtypeStruct((sublanes, width), f32))
        out_specs.append(whole(sublanes, width))
        out_shape.append(jax.ShapeDtypeStruct(rows_shape, f32))
        out_specs.append(whole(*rows_shape))
        out_shape.append(jax.ShapeDtypeStruct((count, 2, part, width), f32))
        out_specs.append(pl.BlockSpec((None, 2, tile, width), lambda t, at: (b, 0, t, 0)))
        scratch.append(pltpu.VMEM((2 * part, lanes), f32))
    if brings is not None or carries is not None:
        add(stats, whole(*stats.shape))
    if brings is not None:
        out_shape.append(jax.ShapeDtypeStruct(stats.shape, f32))
        out_specs.append(whole(*stats.shape))
    moved = part * width * (4 * (2 * slots + 8) + 2 * 8)
    result = pl.pallas_call(
        functools.partial(step_kernel, takes, finishes, b, sends, starts, brings, carries),
        out_shape=out_shape,
        grid_spec=pltpu.PrefetchScalarGridSpec(
            num_scalar_prefetch=1,
            grid=(part // tile,),
            in_specs=in_specs,
            out_specs=out_specs,
            scratch_shapes=scratch,
        ),
        input_output_aliases=aliases,
        compiler_params=params_of(34),
        cost_estimate=pl.CostEstimate(
            flops=part * width * 20, bytes_accessed=moved, transcendentals=0
        ),
        name="step",
    )(me, *operands)
    sent = list(result[:2]) if slots else None
    rest = list(result[2:] if slots else result)
    return sent, rest[:3] if finishes else None, rest[3] if brings is not None else stats


def weighted_kernel(extent, factor, cols, summed, *refs):
    *totals, rows_out, stats, weighted = refs
    count, _, part, width = summed.shape
    total = tree_sum([x[...] for x in totals])
    row_new = decay_rate * factor[...] + (1.0 - decay_rate) * (total / extent + tiny_eps)
    rows_out[...] = row_new
    inverse = jnp.transpose(1.0 / row_new)
    weighted[...] = jnp.zeros_like(weighted)
    for i in range(count):
        for r in range(0, 2 * part, sublanes):
            half, at = divmod(r, part)
            x = summed[i, half, at : at + sublanes]
            weighted[...] += x * x * inverse[r : r + sublanes, i : i + 1]
    size = width // sublanes
    for at, x in ((0, cols), (size, weighted)):
        sums = jnp.sum(x[...], axis=0, keepdims=True)
        for k in range(sublanes):
            stats[k : k + 1, at : at + size] = sums[:, k * size : (k + 1) * size]
    level = jnp.sum(jnp.sum(row_new, axis=0, keepdims=True), axis=1, keepdims=True)
    stats[:, 2 * size :] = jnp.broadcast_to(level, (sublanes, lanes))


def weighted_sums(extent, totals, factor, cols, summed):
    width = summed.shape[-1]
    in_vmem = pl.BlockSpec(memory_space=pltpu.VMEM)
    return pl.pallas_call(
        functools.partial(weighted_kernel, extent),
        in_specs=[in_vmem] * (3 + len(totals)),
        out_specs=[in_vmem] * 2,
        out_shape=[
            jax.ShapeDtypeStruct(totals[0].shape, f32),
            jax.ShapeDtypeStruct((sublanes, 2 * width // sublanes + lanes), f32),
        ],
        scratch_shapes=[pltpu.VMEM((sublanes, width), f32)],
        compiler_params=params_of(16),
        cost_estimate=pl.CostEstimate(
            flops=3 * summed.size, bytes_accessed=4 * summed.size, transcendentals=0
        ),
        name="weighted",
    )(factor.reshape(totals[0].shape), cols, summed, *totals)


def column_kernel(extent, factor, *refs):
    *parts, cols_out, pair, sums = refs
    stats = tree_sum([x[...] for x in parts])
    size = factor.shape[1] // sublanes
    for i in range(2):
        for k in range(sublanes):
            sums[i : i + 1, k * size : (k + 1) * size] = stats[k : k + 1, i * size : (i + 1) * size]
    col_new = decay_rate * factor[...] + (1.0 - decay_rate) * (sums[0:1] / extent + tiny_eps)
    cols_out[...] = col_new
    total = jnp.sum(sums[1:2] / col_new, axis=1, keepdims=True)
    pair[...] = stats[:, 2 * size :] / extent
    pair[0:1] = jnp.broadcast_to(total, (1, lanes))


def column_stage(extent, factor, parts):
    return pl.pallas_call(
        functools.partial(column_kernel, extent),
        in_specs=[pl.BlockSpec(memory_space=pltpu.VMEM)] * (1 + len(parts)),
        out_specs=[pl.BlockSpec(memory_space=pltpu.VMEM)] * 2,
        out_shape=[
            jax.ShapeDtypeStruct(factor.shape, f32),
            jax.ShapeDtypeStruct((sublanes, lanes), f32),
        ],
        scratch_shapes=[pltpu.VMEM((sublanes, factor.shape[1]), f32)],
        compiler_params=params_of(4),
        name="column",
    )(factor, *parts)


def finish_kernel(m, extent, partners, staged, row_new, col_new, summed, params, *refs):
    pairs, (new_params, update, column, by_col) = refs[:partners], refs[-4:]
    count, _, part, width = summed.shape

    def scale():
        row_level = pairs[0][1:2, 0:1]
        total = tree_sum([x[0:1, 0:1] for x in pairs]) * row_level
        spread = jnp.sqrt(total / (extent * extent))
        factor = jnp.sqrt(row_level) / jnp.maximum(1.0, spread / clip_limit)
        by_row = jnp.transpose(lax.rsqrt(row_new[...]) * factor)
        for i in range(count):
            column[i] = jnp.broadcast_to(by_row[:, i : i + 1], column.shape[1:])
        by_col[...] = lax.rsqrt(col_new[...])

    def body(*blocks):
        new_p, moved = blocks[-2:]
        pl.when(pl.program_id(0) == 0)(scale)
        for g, half, r in itertools.product(range(2), range(2), range(0, part, sublanes)):
            i = 2 * pl.program_id(0) + g
            rows = slice(r, r + sublanes)
            at = half * part + r
            y = summed[i, half, rows] * column[i, at : at + sublanes][:, 0:1] * by_col[...]
            moved[g, half, rows] = y
            p = params[i, half, rows] if staged else blocks[0][g, half, rows]
            new_p[g, half, rows] = p - learn_rate * y

    of_matrix = pl.BlockSpec((None, 2, 2, part, width), lambda i: (m, i, 0, 0, 0))
    pltpu.emit_pipeline(
        body, grid=(count // 2,), in_specs=[] if staged else [of_matrix], out_specs=[of_matrix] * 2
    )(*([] if staged else [params]), new_params, update)


def finish(m, extent, row_new, col_new, pairs, summed, params, outs, mib):
    count, _, part, width = summed.shape
    held = () if outs is None else outs
    staged = params.ndim == summed.ndim
    in_hbm = pl.BlockSpec(memory_space=pltpu.HBM)
    in_vmem = pl.BlockSpec(memory_space=pltpu.VMEM)
    return pl.pallas_call(
        functools.partial(finish_kernel, m, extent, len(pairs), staged),
        in_specs=[in_vmem] * 3
        + [in_vmem if staged else in_hbm]
        + [in_vmem] * len(pairs)
        + [in_hbm] * len(held),
        out_specs=[in_hbm] * 2,
        out_shape=[jax.ShapeDtypeStruct(held[0].shape if staged else params.shape, f32)] * 2,
        scratch_shapes=[
            pltpu.VMEM((count, 2 * part, lanes), f32),
            pltpu.VMEM((1, width), f32),
        ],
        input_output_aliases={4 + len(pairs) + i: i for i in range(len(held))},
        compiler_params=params_of(mib),
        cost_estimate=pl.CostEstimate(
            flops=4 * summed.size, bytes_accessed=16 * summed.size, transcendentals=0
        ),
        name="finish",
    )(row_new, col_new, summed, params, *pairs, *held)


def per_device(partials, params, row_factor, col_factor):
    mats, rows, block_cols = params.shape
    extent = block_cols * lax.axis_size("col")
    me = lax.axis_index("dp").astype(jnp.int32).reshape(1)
    count = blocks_of_matrix
    part = rows // (2 * count)
    total_blocks = mats * count
    pieces = partials.reshape(mats, partials.shape[2], count, 2, part, block_cols)
    blocked = params.reshape(mats, count, 2, part, block_cols)
    new_rows, new_columns = [], []

    def row_stage(m, sums):
        cols, rows_along, summed = sums
        row_new, stats = weighted_sums(
            extent, exchange(rows_along, "col"), row_factor[m], cols, summed
        )
        new_rows.append(row_new.reshape(rows))
        return row_new, pairwise_sum(stats, "row")

    def col_stage(m, parts):
        col_new, pair = column_stage(extent, col_factor[m : m + 1], parts)
        new_columns.append(col_new)
        return col_new, exchange(pair, "col")

    flying = {}
    sums = stats = outs = None
    last = {}
    for j in range(-2, total_blocks + 2):
        m, b = divmod(j - 2, count)
        since = b + 1 if m >= 1 else None
        carries = {1: 0, 3: 1}.get(since)
        brings = {3: 0, 5: 1}.get(since)
        got = flying.pop(j, None)
        sent, sums, stats = step(
            j, total_blocks, me, pieces, got, sums, stats, brings, carries
        )
        if sent is not None:
            flying[j + 2] = [swap(sent[0], "dp", 1), swap(sent[1], "dp", 2)]
        if sums:
            me, *sums = tie(me, *sums)
        else:
            me, *_ = tie(me, *sent)
        if 0 <= m < mats - 1 and b == count - 1:
            row_new, stats = row_stage(m, sums)
            last = dict(m=m, row_new=row_new, summed=sums[2])
            me, stats = tie(me, stats)
        if since == 5:
            stats, me = tie(stats, me)
            col_new, pairs = col_stage(last["m"], [stats])
            outs = finish(
                last["m"], extent, last["row_new"], col_new, pairs, last["summed"], blocked, outs, 36
            )
            me, *outs = tie(me, *outs)
        if j == total_blocks - 1:
            me, last_params = tie(me, blocked[mats - 1])
    row_new, stats = row_stage(mats - 1, sums)
    col_new, pairs = col_stage(mats - 1, exchange(stats, "dp"))
    new_params, update = finish(
        mats - 1, extent, row_new, col_new, pairs, sums[2], last_params, outs, 12
    )
    return (
        new_params.reshape(params.shape),
        update.reshape(params.shape),
        jnp.stack(new_rows),
        jnp.concatenate(new_columns, axis=0),
    )


def solution(mesh):
    placed = (
        P("dp", None, None, "row", None, "col"),
        P(None, ("dp", "row"), "col"),
        P(None, ("dp", "row")),
        P(None, "col"),
    )
    return jax.shard_map(
        per_device,
        mesh=mesh,
        in_specs=placed,
        out_specs=(
            P(None, ("dp", "row"), "col"),
            P(None, ("dp", "row"), "col"),
            P(None, ("dp", "row")),
            P(None, "col"),
        ),
        check_vma=False,
    )
```
